32 devices in a mesh: fsdp: 8 (over z, core), tp: 4 (over y, x).
Axes of the slice: x: 2, y: 2, z: 4, core: 2. Of those that a mesh axis runs over, the one named last changes fastest.
Arguments:
- tokens: bfloat16 [8192, 2048], P(('fsdp', 'tp')), may hold values from -6 to 6
- cotangent: bfloat16 [8192, 2048], P(('fsdp', 'tp')), may hold values from -6 to 6
- routes: int32 [8192, 8], P('fsdp'), may hold values from 0 to 31, all different within a row; in each aligned block of 1024 rows (0 to 1023, 1024 to 2047, ...) at most 320 rows name the same one
- gain_attn: bfloat16 [2048], P('fsdp'), may hold values from 0.099609375 to 1.8984375
- w_query: bfloat16 [2048, 2048], P('fsdp', 'tp'), may hold values from -0.125 to 0.125
- w_key: bfloat16 [2048, 2048], P('fsdp', 'tp'), may hold values from -0.125 to 0.125
- w_value: bfloat16 [2048, 2048], P('fsdp', 'tp'), may hold values from -0.125 to 0.125
- gain_query: bfloat16 [2048], P('fsdp'), may hold values from 0.099609375 to 1.8984375
- gain_key: bfloat16 [2048], P('fsdp'), may hold values from 0.099609375 to 1.8984375
- w_out: bfloat16 [2048, 2048], P('tp', 'fsdp'), may hold values from -1 to 1
- gain_moe: bfloat16 [2048], P('fsdp'), may hold values from 0.099609375 to 1.8984375
- w_router: bfloat16 [2048, 32], P('fsdp'), may hold values from -0.0625 to 0.0625
- w_gate: bfloat16 [32, 2048, 1024], P('fsdp', None, 'tp'), may hold values from -0.125 to 0.125
- w_up: bfloat16 [32, 2048, 1024], P('fsdp', None, 'tp'), may hold values from -0.125 to 0.125
- w_down: bfloat16 [32, 1024, 2048], P('fsdp', 'tp'), may hold values from -4 to 4
Outputs:
- output: bfloat16 [8192, 2048], P(('fsdp', 'tp'))
- grad_tokens: float32 [8192, 2048], P(('fsdp', 'tp'))
- grad_gain_attn: float32 [2048], P('fsdp')
- grad_w_query: float32 [2048, 2048], P('fsdp', 'tp')
- grad_w_key: float32 [2048, 2048], P('fsdp', 'tp')
- grad_w_value: float32 [2048, 2048], P('fsdp', 'tp')
- grad_gain_query: float32 [2048], P('fsdp')
- grad_gain_key: float32 [2048], P('fsdp')
- grad_w_out: float32 [2048, 2048], P('tp', 'fsdp')
- grad_gain_moe: float32 [2048], P('fsdp')
- grad_w_router: float32 [2048, 32], P('fsdp')
- grad_w_gate: float32 [32, 2048, 1024], P('fsdp', None, 'tp')
- grad_w_up: float32 [32, 2048, 1024], P('fsdp', None, 'tp')
- grad_w_down: float32 [32, 1024, 2048], P('fsdp', 'tp')
The draws below stay inside these ranges and needn't reach their ends.
Inputs may be any that keep to these rules, and one draw needn't show every extreme that they name: `routes`: within the 1024 rows of one index of fsdp (one aligned block), each row names 8 different experts and no expert is named by more than 320 rows; some expert is named by exactly 320 rows in some block of every draw.
All inputs are finite; a program needn't handle non-finite values.
Results may differ from the reference program's by a relative error of at most 0.02.
Values may be sent and summed in bfloat16 or wider, within the bound.
No kernel may reach another device: no remote copies, remote signals or barrier semaphores. Data moves between devices by JAX's collectives and lax.ppermute only.
A program may use at most 512 MiB of HBM per device.

```python
import math
import jax
import jax.numpy as jnp
import numpy as np
from jax import lax

D = 2048
HEADS = 16
HEAD_DIM = 128
FF = 1024
TOPK = 8
SEQ = 1024
EXPERTS = 32
TOKENS = 8192
CAP = 320
N_FSDP = 8


def steps_of(stream_key, shape, split, low, top_value):
    def one(position, blocks):
        heights = jax.random.uniform(jax.random.fold_in(jax.random.fold_in(stream_key, 6), position), (blocks,), jnp.float32, low / len(split), top_value / len(split))
        return jnp.repeat(jnp.exp(heights), shape[position] // blocks).reshape((-1,) + (1,) * (len(shape) - position - 1))

    loudness = one(*split[0])
    for cut in split[1:]:
        loudness = loudness * one(*cut)
    return loudness


def shared_out(own_key, own, number, rows, amount, top, bound, skew):
    ranking = jax.random.permutation(own_key, amount)
    crowded, usual = portions_of(amount, rows * top, bound, skew, True), portions_of(amount, rows * top, bound, skew, False)
    places = jnp.arange(amount)

    def named(sizes, offset_by):
        used = int((sizes > 0).sum())
        fixed = max(1, used // 4)
        passed = fixed + (places - fixed + offset_by * (used - fixed)) % max(1, amount - fixed)
        return jnp.zeros((amount,), jnp.int32).at[ranking[jnp.where(places < fixed, places, passed)]].set(jnp.asarray(sizes, jnp.int32))

    sizes = jnp.where(number % 4 == 0, named(crowded, number // 4), named(usual, number - number // 4 - 1))
    mixed = jax.random.permutation(jax.random.fold_in(own, 3), amount)
    donor, sink = mixed[0:amount // 2 * 2:2], mixed[1:amount // 2 * 2:2]
    slack = jnp.minimum(sizes[donor] - 1, bound - sizes[sink]) // 2
    slack = jnp.where((donor == ranking[0]) | (sink == ranking[0]) | (sizes[sink] == 0), 0, jnp.maximum(slack, 0))
    passed = jax.random.randint(jax.random.fold_in(own, 4), (amount // 2,), 0, 1 << 20) % (slack + 1)
    sizes = sizes.at[donor].add(-passed).at[sink].add(passed)
    labels = jnp.searchsorted(jnp.cumsum(sizes), jnp.arange(rows * top), side="right").astype(jnp.int32)
    grid = labels.reshape(top, rows).T
    grid = grid[jax.random.permutation(jax.random.fold_in(own, 1), rows)]
    offset_by = jax.random.randint(jax.random.fold_in(own, 2), (rows, 1), 0, top)
    return jnp.take_along_axis(grid, (jnp.arange(top)[None, :] + offset_by) % top, axis=1)


def portions_of(amount, total, limit, slope, full):
    loads = [(1 << 20) // math.isqrt(standing ** slope) + 1 for standing in range(1, amount + 1)]
    largest = limit if full else min(limit, max(-(-total // amount), total * loads[0] // sum(loads)))
    least = 1 if total - largest >= amount - 1 else 0
    given, spare = [largest] + [least] * (amount - 1), total - largest - least * (amount - 1)
    while spare > 0:
        free = [i for i in range(1, amount) if given[i] < largest] or [i for i in range(1, amount) if given[i] < limit]
        whole, left = sum([loads[i] for i in free]), spare
        for i in free:
            more = min(limit - given[i], max(1, left * loads[i] // whole), spare)
            given[i] = given[i] + more
            spare = spare - more
    return np.array(given)


def centred(rng, shape, deviation, limit, split=(), kind=jnp.bfloat16):
    drawn = jax.random.normal(rng, shape, jnp.float32) * deviation
    if len(split) > 0:
        drawn = steps_of(rng, shape, split, -0.22, 0.18) * drawn
    return jnp.clip(drawn, min=-limit, max=limit).astype(kind)


def setup_inputs(seed: int = 0) -> dict:
    arg_keys = jax.random.split(jax.random.key(seed), 16)
    tokens = centred(arg_keys[0], (TOKENS, D), 1.0, 6.0, ((0, 32),))
    cotangent = centred(arg_keys[1], (TOKENS, D), 1.0, 6.0, ((0, 32),))
    routes_keys = jax.random.split(jax.random.fold_in(arg_keys[2], 1), TOKENS // SEQ)
    routes_turns = jax.random.permutation(jax.random.fold_in(arg_keys[2], 3), TOKENS // SEQ)
    routes = jax.vmap(lambda own, number: shared_out(jax.random.fold_in(arg_keys[2], 2), own, number, SEQ, EXPERTS, TOPK, CAP, 1))(routes_keys, routes_turns).reshape((TOKENS, TOPK))
    gain_attn = jnp.clip(1.0 + 0.18 * jax.random.normal(arg_keys[3], (D,), jnp.float32), 0.099609375, 1.8984375).astype(jnp.bfloat16)
    w_query = centred(arg_keys[4], (D, D), D ** -0.5, 0.125, ((0, 8), (1, 4)))
    w_key = centred(arg_keys[5], (D, D), D ** -0.5, 0.125, ((0, 8), (1, 4)))
    w_value = centred(arg_keys[6], (D, D), D ** -0.5, 0.125, ((0, 8), (1, 4)))
    gain_query = jnp.clip(1.0 + 0.18 * jax.random.normal(arg_keys[7], (D,), jnp.float32), 0.099609375, 1.8984375).astype(jnp.bfloat16)
    gain_key = jnp.clip(1.0 + 0.18 * jax.random.normal(arg_keys[8], (D,), jnp.float32), 0.099609375, 1.8984375).astype(jnp.bfloat16)
    w_out = centred(arg_keys[9], (D, D), (D // 64) ** -0.5, 1.0, ((0, 4), (1, 8)))
    gain_moe = jnp.clip(1.0 + 0.18 * jax.random.normal(arg_keys[10], (D,), jnp.float32), 0.099609375, 1.8984375).astype(jnp.bfloat16)
    w_router = centred(arg_keys[11], (D, EXPERTS), (4 * D) ** -0.5, 0.0625, ((0, 8),))
    w_gate = centred(arg_keys[12], (EXPERTS, D, FF), D ** -0.5, 0.125, ((0, 8), (2, 4)))
    w_up = centred(arg_keys[13], (EXPERTS, D, FF), D ** -0.5, 0.125, ((0, 8), (2, 4)))
    w_down = centred(arg_keys[14], (EXPERTS, FF, D), (max(FF // 512, 1)) ** -0.5, 4.0, ((0, 8), (1, 4)))
    return {"tokens": tokens, "cotangent": cotangent, "routes": routes, "gain_attn": gain_attn, "w_query": w_query, "w_key": w_key, "w_value": w_value, "gain_query": gain_query, "gain_key": gain_key, "w_out": w_out, "gain_moe": gain_moe, "w_router": w_router, "w_gate": w_gate, "w_up": w_up, "w_down": w_down}


EPSILON = 1e-05
ROPE_BASE = 10000.0

@jax.custom_vjp
def low(v):
    return lax.optimization_barrier(v.astype(jnp.bfloat16)).astype(jnp.float32)

@jax.custom_vjp
def low_back(v):
    return v

def low_keep(v):
    return (low(v), None)

def low_pass(kept, grad):
    return (grad,)

def back_keep(v):
    return (v, None)

def back_low(kept, grad):
    return (low(grad),)
low.defvjp(low_keep, low_pass)
low_back.defvjp(back_keep, back_low)

def product(first, second):
    return jnp.dot(first, second, precision=lax.Precision.HIGHEST)

def normalize(tensor):
    return tensor * lax.rsqrt(lax.optimization_barrier(jnp.mean(tensor * tensor, axis=-1, keepdims=True)) + EPSILON)

def rope_tables(length, columns):
    halfway = columns // 2
    positions = jnp.arange(length).astype(jnp.float32)
    frequency = ROPE_BASE ** (-2.0 * jnp.arange(halfway).astype(jnp.float32) / columns)
    angles = positions[:, None] * frequency[None, :]
    angles = jnp.concatenate([angles, angles], axis=-1)
    return (jnp.cos(angles)[:, None, :], jnp.sin(angles)[:, None, :])

def rotate(tensor):
    halfway = tensor.shape[-1] // 2
    return jnp.concatenate([-tensor[..., halfway:], tensor[..., :halfway]], axis=-1)

def apply_rope(tensor, cosine, sine_table):
    return tensor * cosine + rotate(tensor) * sine_table

def attend(operands):
    query_rows, key_rows, value_rows = operands
    length = query_rows.shape[0]
    scores = jnp.einsum('qhd,khd->hqk', query_rows, key_rows, precision=lax.Precision.HIGHEST) * HEAD_DIM ** (-0.5)
    scores = low_back(scores)
    causal = jnp.arange(length)[:, None] >= jnp.arange(length)[None, :]
    scores = jnp.where(causal[None], scores, -1e+30)
    attn_probs = low(jax.nn.softmax(scores, axis=-1))
    return jnp.einsum('hqk,khd->qhd', attn_probs, value_rows, precision=lax.Precision.HIGHEST)

def reference(tokens, cotangent, routes, gain_attn, w_query, w_key, w_value, gain_query, gain_key, w_out, gain_moe, w_router, w_gate, w_up, w_down):
    slot_total = EXPERTS * N_FSDP * CAP
    grouped = routes.reshape(N_FSDP, SEQ * TOPK)
    onehot = (grouped[:, :, None] == jnp.arange(EXPERTS, dtype=jnp.int32)[None, None, :]).astype(jnp.int32)
    slot_rank = lax.optimization_barrier(jnp.sum(onehot * (jnp.cumsum(onehot, axis=1) - 1), axis=-1))
    group_base = (jnp.arange(N_FSDP, dtype=jnp.int32) * CAP)[:, None]
    slot_index = (grouped * (N_FSDP * CAP) + group_base + slot_rank).reshape(-1).astype(jnp.int32)
    token_index = jnp.arange(TOKENS * TOPK, dtype=jnp.int32) // TOPK
    token_of = jnp.full((slot_total,), TOKENS, jnp.int32).at[slot_index].set(token_index)

    def forward(residual_in, attn_gain, query_w, key_w, value_w, query_gain, key_gain, out_w, moe_gain, router_w, gate_w, up_w, down_w):
        first_in = low(normalize(residual_in) * attn_gain)
        query_raw = low_back(product(first_in, query_w))
        key_raw = low_back(product(first_in, key_w))
        value_raw = low_back(low(product(first_in, value_w)))
        head_shape = (N_FSDP, SEQ, HEADS, HEAD_DIM)
        cosine, sine_table = rope_tables(SEQ, HEAD_DIM)
        query_rot = low(apply_rope((normalize(query_raw) * query_gain).reshape(head_shape), cosine, sine_table))
        key_rot = low(apply_rope((normalize(key_raw) * key_gain).reshape(head_shape), cosine, sine_table))
        attended = lax.map(jax.checkpoint(attend), (query_rot, key_rot, value_raw.reshape(head_shape)))
        heads_out = low_back(low(attended.reshape(TOKENS, D)))
        hidden_res = residual_in + low_back(product(heads_out, out_w))
        second_in = low(normalize(hidden_res) * moe_gain)
        router_probs = jax.nn.softmax(product(second_in, router_w), axis=-1)
        gate_values = jnp.take_along_axis(router_probs, routes, axis=1)
        gate_of = jnp.zeros((slot_total,), jnp.float32).at[slot_index].set(gate_values.reshape(-1))
        padded_in = jnp.concatenate([second_in, jnp.zeros((1, D), jnp.float32)], axis=0)

        def expert(operands):
            token_rows, gate_one, up_one, down_one = operands
            expert_rows = padded_in[token_rows]
            gate_pre = low_back(product(expert_rows, gate_one))
            up_pre = low_back(product(expert_rows, up_one))
            expert_hidden = low(jax.nn.silu(gate_pre) * up_pre)
            return low_back(product(expert_hidden, down_one))
        expert_out = lax.map(jax.checkpoint(expert), (token_of.reshape(EXPERTS, N_FSDP * CAP), gate_w, up_w, down_w))
        weighted = expert_out.reshape(slot_total, D) * gate_of[:, None]
        moe_sum = jnp.zeros((TOKENS + 1, D), jnp.float32).at[token_of].add(weighted)[:TOKENS]
        return hidden_res + moe_sum
    primals = (tokens.astype(jnp.float32), gain_attn.astype(jnp.float32), w_query.astype(jnp.float32), w_key.astype(jnp.float32), w_value.astype(jnp.float32), gain_query.astype(jnp.float32), gain_key.astype(jnp.float32), w_out.astype(jnp.float32), gain_moe.astype(jnp.float32), w_router.astype(jnp.float32), w_gate.astype(jnp.float32), w_up.astype(jnp.float32), w_down.astype(jnp.float32))
    result, pullback = jax.vjp(forward, *primals)
    gradients = pullback(cotangent.astype(jnp.float32))
    return (result.astype(jnp.bfloat16), gradients[0], gradients[1], gradients[2], gradients[3], gradients[4], gradients[5], gradients[6], gradients[7], gradients[8], gradients[9], gradients[10], gradients[11], gradients[12])
```

```python
import functools

import jax
import jax.numpy as jnp
from jax import lax
from jax.experimental import pallas as pl
from jax.experimental.pallas import tpu as pltpu
from jax.sharding import PartitionSpec as P

HEAD_DIM = 128
EPSILON = 1e-05
ROPE_BASE = 10000.0
F32 = jnp.float32
BF16 = jnp.bfloat16


def dot(a, b):
    return jnp.dot(a, b, preferred_element_type=F32)


def dot_nt(a, b):
    return lax.dot_general(a, b, (((1,), (1,)), ((), ())), preferred_element_type=F32)


def dot_tn(a, b):
    return lax.dot_general(a, b, (((0,), (0,)), ((), ())), preferred_element_type=F32)


def swap_core(operand):
    count = lax.axis_size("fsdp")
    return lax.ppermute(operand, "fsdp", [(i, i ^ 1) for i in range(count)])


def shift_node(operand, step):
    count = lax.axis_size("fsdp")
    nodes = count // 2
    if step % nodes == 0:
        return operand
    return lax.ppermute(
        operand, "fsdp", [(i, ((i // 2 + step) % nodes) * 2 + i % 2) for i in range(count)]
    )


def around_nodes(operand):
    count = lax.axis_size("fsdp") // 2
    pieces = []
    for step in range(1, count - 1):
        pieces.append(shift_node(pieces[-1] if pieces else operand, 1))
    if count > 1:
        pieces.append(shift_node(operand, -1))
    return pieces


def swap_tp(operand, mask):
    count = lax.axis_size("tp")
    return lax.ppermute(operand, "tp", [(i, i ^ mask) for i in range(count)])


def after(operand, *earlier):
    return lax.optimization_barrier((operand,) + earlier)[0]


def gather_halves(operand):
    if lax.axis_size("tp") != 4:
        return lax.all_gather(operand, "tp", axis=0, tiled=True)
    rows = operand.shape[0]
    half = rows // 2
    a, b = operand[:half], operand[half:]
    a1 = swap_tp(a, 1)
    b2 = swap_tp(b, 2)
    b1 = swap_tp(b, 1)
    a2 = swap_tp(a, 2)
    a3 = swap_tp(a1, 2)
    b3 = swap_tp(b2, 1)
    rank = lax.axis_index("tp")
    placed = jnp.zeros((4 * rows,) + operand.shape[1:], operand.dtype)
    for mask, part, offset in (
        (0, operand, 0),
        (1, a1, 0),
        (1, b1, half),
        (2, a2, 0),
        (2, b2, half),
        (3, a3, 0),
        (3, b3, half),
    ):
        placed = lax.dynamic_update_slice_in_dim(placed, part, (rank ^ mask) * rows + offset, 0)
    return placed


def plus(mine, other):
    return mine.astype(F32) + other.astype(F32)


def hop_one(operand, other=None):
    rows = operand.shape[0] // 4
    half = rows // 2
    rank = lax.axis_index("tp")

    def part(mask, offset):
        start = (rank ^ mask) * rows + offset
        mine = lax.dynamic_slice_in_dim(operand, start, half, 0)
        if other is None:
            return mine
        return plus(mine, lax.dynamic_slice_in_dim(other, start, half, 0))

    arrived = (
        swap_tp(part(3, 0).astype(BF16), 2),
        swap_tp(part(3, half).astype(BF16), 1),
        swap_tp(part(2, 0).astype(BF16), 2),
        swap_tp(part(1, half).astype(BF16), 1),
    )
    return part, half, arrived


def hop_two(part, half, arrived):
    a3, b3, _, _ = arrived
    return (
        swap_tp(plus(part(1, 0), a3).astype(BF16), 1),
        swap_tp(plus(part(2, half), b3).astype(BF16), 2),
    )


def hop_sum(part, half, arrived, last):
    _, _, a2, b1 = arrived
    ra = plus(plus(part(0, 0), a2), last[0])
    rb = plus(plus(part(0, half), b1), last[1])
    return jnp.concatenate([ra, rb], axis=0)


def scatter_halves(operand):
    if lax.axis_size("tp") != 4:
        return lax.psum_scatter(operand, "tp", scatter_dimension=0, tiled=True).astype(F32)
    first = hop_one(operand)
    return hop_sum(*first, hop_two(*first))


def gather_small(operand):
    count = lax.axis_size("fsdp")
    nodes = count // 2
    rank = lax.axis_index("fsdp")
    node, core = rank // 2, rank % 2
    other = swap_core(operand)
    pair = jnp.where(core == 0, jnp.stack([operand, other]), jnp.stack([other, operand]))
    around = [shift_node(pair, step) for step in range(nodes - 1, 0, -1)] + [pair]
    both = jnp.concatenate(around + around, axis=0)
    placed = lax.dynamic_slice_in_dim(both, 2 * (nodes - 1 - node), count, 0)
    return placed.transpose(1, 0, 2).reshape(operand.shape[0], -1)


def reduce_small(operand):
    count = lax.axis_size("fsdp")
    nodes = count // 2
    rank = lax.axis_index("fsdp")
    node, core = rank // 2, rank % 2
    blocks = operand.reshape(operand.shape[0], nodes, 2, -1).transpose(2, 1, 0, 3)
    mine = lax.dynamic_index_in_dim(blocks, core, 0, keepdims=False)
    mine = mine + swap_core(lax.dynamic_index_in_dim(blocks, 1 - core, 0, keepdims=False))
    total = lax.dynamic_index_in_dim(mine, node, 0, keepdims=False)
    for step in range(1, nodes):
        part = lax.dynamic_index_in_dim(mine, (node + step) % nodes, 0, keepdims=False)
        total = total + shift_node(part, step)
    return sum_tp(total)


def sum_tp(operand):
    if lax.axis_size("tp") != 4:
        return lax.psum(operand, "tp")
    return (operand + swap_tp(operand, 1)) + (swap_tp(operand, 2) + swap_tp(operand, 3))


def rope_tables(positions, columns):
    halfway = columns // 2
    frequency = ROPE_BASE ** (-2.0 * jnp.arange(halfway).astype(F32) / columns)
    angles = positions.astype(F32)[:, None] * frequency[None, :]
    angles = jnp.concatenate([angles, angles], axis=-1)
    return (jnp.cos(angles)[:, None, :], jnp.sin(angles)[:, None, :])


def rotate(tensor):
    halfway = tensor.shape[-1] // 2
    return jnp.concatenate([-tensor[..., halfway:], tensor[..., :halfway]], axis=-1)


def rotate_back(tensor):
    halfway = tensor.shape[-1] // 2
    return jnp.concatenate([tensor[..., halfway:], -tensor[..., :halfway]], axis=-1)


def norm_rows(tensor):
    row_scale = lax.rsqrt(jnp.mean(tensor * tensor, axis=-1, keepdims=True) + EPSILON)
    return (tensor * row_scale, row_scale)


def norm_back(normed, row_scale, grad_normed):
    return row_scale * (
        grad_normed - normed * jnp.mean(normed * grad_normed, axis=-1, keepdims=True)
    )


def expert_kernel(extra, experts, base, *refs):
    x_ref, z_ref, gate_w, up_w, down_w = refs[:5]
    back_ref, out_ref, dots_ref, hidden_ref, gate_grad_ref, up_grad_ref, copy_ref = refs[-7:]
    count, width, size = gate_w.shape
    x = x_ref[:, :width]
    copy_ref[0] = x
    ends = x_ref[:, width:].astype(F32)
    lane = lax.broadcasted_iota(jnp.int32, ends.shape, 1)
    dots = jnp.zeros(ends.shape, F32)
    for e in range(count):
        columns = slice(e * size, (e + 1) * size)
        number = base[0] + e
        gate = jnp.sum(
            jnp.where((lane == number) | (lane == number + experts), ends, 0.0),
            axis=1,
            keepdims=True,
        )
        gate_pre = dot(x, gate_w[e])
        up_pre = dot(x, up_w[e])
        down_grad = z_ref[:, columns].astype(F32)
        sigmoid_gate = 1.0 / (1.0 + jnp.exp(-gate_pre))
        activated = gate_pre * sigmoid_gate
        hidden = activated * up_pre
        hidden_ref[0, :, columns] = (hidden * gate).astype(BF16)
        dots = dots + jnp.where(
            lane == number, jnp.sum(hidden * down_grad, axis=1, keepdims=True), 0.0
        )
        hidden_grad = down_grad * gate
        gate_grad_ref[0, :, columns] = (
            hidden_grad * up_pre * sigmoid_gate * (1.0 + gate_pre * (1.0 - sigmoid_gate))
        ).astype(BF16)
        up_grad_ref[0, :, columns] = (hidden_grad * activated).astype(BF16)
    dots_ref[...] = dots
    tile = min(512, width)
    for start in range(0, width, tile):
        rows = slice(start, start + tile)
        back = jnp.zeros((x.shape[0], tile), F32)
        out = jnp.zeros((x.shape[0], tile), F32)
        for e in range(count):
            columns = slice(e * size, (e + 1) * size)
            back = back + dot_nt(gate_grad_ref[0, :, columns], gate_w[e, rows, :])
            back = back + dot_nt(up_grad_ref[0, :, columns], up_w[e, rows, :])
            out = out + dot(hidden_ref[0, :, columns], down_w[e, :, rows])
        back_ref[:, rows] = back.astype(BF16)
        out_ref[:, rows] = out.astype(BF16)


def expert_products(base, x, z, gate_w, up_w, down_w, slots, slot, kept, experts):
    rows, wide = x.shape
    count, width, size = gate_w.shape
    extra = wide - width
    block = min(512, rows)
    hidden = count * size

    def whole(array):
        return pl.BlockSpec(
            array.shape, lambda i, base: (0, 0, 0), pipeline_mode=pl.Buffered(1)
        )

    def by_rows(columns):
        return pl.BlockSpec((block, columns), lambda i, base: (i, 0))

    def in_slot(columns):
        return pl.BlockSpec((1, block, columns), lambda i, base: (slot, i, 0))

    kept_shapes = [
        jax.ShapeDtypeStruct((slots, rows, columns), BF16)
        for columns in (hidden, hidden, hidden, width)
    ]
    results = pl.pallas_call(
        functools.partial(expert_kernel, extra, experts),
        out_shape=[
            jax.ShapeDtypeStruct((rows, width), BF16),
            jax.ShapeDtypeStruct((rows, width), BF16),
            jax.ShapeDtypeStruct((rows, extra), F32),
        ]
        + kept_shapes,
        grid_spec=pltpu.PrefetchScalarGridSpec(
            num_scalar_prefetch=1,
            grid=(rows // block,),
            in_specs=[by_rows(wide), by_rows(hidden), whole(gate_w), whole(up_w), whole(down_w)]
            + [pl.BlockSpec(memory_space=pl.ANY)] * len(kept),
            out_specs=[by_rows(width), by_rows(width), by_rows(extra)]
            + [in_slot(columns) for columns in (hidden, hidden, hidden, width)],
        ),
        input_output_aliases={6 + i: 3 + i for i in range(len(kept))},
        cost_estimate=pl.CostEstimate(
            flops=10 * rows * width * hidden,
            bytes_accessed=6 * width * hidden + 2 * rows * (4 * width + 4 * hidden),
            transcendentals=rows * hidden,
        ),
        compiler_params=pltpu.CompilerParams(vmem_limit_bytes=60 * 1024 * 1024),
    )(base, x, z, gate_w, up_w, down_w, *kept)
    return results[0], results[1], results[2], tuple(results[3:])


def shards(
    tokens,
    cotangent,
    routes,
    gain_attn,
    w_query,
    w_key,
    w_value,
    gain_query,
    gain_key,
    w_out,
    gain_moe,
    w_router,
    w_gate,
    w_up,
    w_down,
):
    tp_count = lax.axis_size("tp")
    tp_rank = lax.axis_index("tp")
    fsdp_count = lax.axis_size("fsdp")
    fsdp_rank = lax.axis_index("fsdp")
    nodes = fsdp_count // 2
    piece, model_width = tokens.shape
    seq_len = piece * tp_count
    local_width = w_query.shape[1]
    head_count = local_width // HEAD_DIM
    expert_count = w_router.shape[1]
    local_experts, _, hidden_slice = w_gate.shape
    hidden_all = local_experts * hidden_slice
    extra = -(-2 * expert_count // 128) * 128
    scale_factor = HEAD_DIM ** (-0.5)
    head_shape = (seq_len, head_count, HEAD_DIM)
    column_start = tp_rank * local_width

    small = gather_small(
        jnp.concatenate(
            [gain_attn[None], gain_moe[None], gain_query[None], gain_key[None], w_router.T], axis=0
        )
    )
    attn_gain, moe_gain = small[0].astype(F32), small[1].astype(F32)
    local_gains = lax.dynamic_slice_in_dim(small[2:4], column_start, local_width, 1).astype(F32)
    local_qgain, local_kgain = local_gains[0], local_gains[1]
    router_w = small[4:]
    qkv_w = lax.all_gather(
        jnp.concatenate([w_query, w_key, w_value], axis=1), "fsdp", axis=0, tiled=True
    )

    down_w = w_down.reshape(hidden_all, model_width)

    residual_in = tokens.astype(F32)
    normed_one, scale_one = norm_rows(residual_in)
    first_in = (normed_one * attn_gain).astype(BF16)
    first_all = gather_halves(first_in)

    early = after(cotangent, qkv_w, first_all)
    grad_own = lax.all_gather(early, "tp", axis=0, tiled=True)
    out_w = lax.all_gather(after(w_out, first_all), "fsdp", axis=1, tiled=True)
    around = around_nodes(early)
    near, far = around[:1] + around[2:], around[1:2]

    qkv_raw = dot(first_all, qkv_w)
    query_raw = qkv_raw[:, :local_width]
    key_raw = qkv_raw[:, local_width : 2 * local_width]
    value_raw = qkv_raw[:, 2 * local_width :]
    squares = sum_tp(
        jnp.stack([jnp.sum(query_raw * query_raw, axis=-1), jnp.sum(key_raw * key_raw, axis=-1)])
    )
    query_scale = lax.rsqrt(squares[0] / model_width + EPSILON)[:, None]
    key_scale = lax.rsqrt(squares[1] / model_width + EPSILON)[:, None]
    positions = jnp.arange(seq_len, dtype=jnp.int32)
    cosine, sine_table = rope_tables(positions, HEAD_DIM)
    query_normed = (query_raw * query_scale * local_qgain).reshape(head_shape)
    key_normed = (key_raw * key_scale * local_kgain).reshape(head_shape)
    query_bf = (query_normed * cosine + rotate(query_normed) * sine_table).astype(BF16)
    key_bf = (key_normed * cosine + rotate(key_normed) * sine_table).astype(BF16)
    value_bf = value_raw.astype(BF16).reshape(head_shape)
    block_rows = min(512, seq_len)
    block_count = seq_len // block_rows

    def block_of(array, block_index):
        return array[block_index * block_rows : (block_index + 1) * block_rows]

    def block_scores(block_index):
        query_block = block_of(query_bf, block_index)
        scores = (
            jnp.einsum("qhd,khd->hqk", query_block, key_bf, preferred_element_type=F32)
            * scale_factor
        )
        causal = block_of(positions, block_index)[:, None] >= positions[None, :]
        return (query_block, jnp.where(causal[None], scores, -1e30), causal)

    attn_blocks, log_totals = [], []
    for block_index in range(block_count):
        query_block, scores, causal = block_scores(block_index)
        if block_index > 0:
            scores = after(scores, near[0])
        top_score = jnp.max(scores, axis=-1, keepdims=True)
        exponent = jnp.exp(scores - top_score)
        row_total = jnp.sum(exponent, axis=-1, keepdims=True)
        attn_probs = (exponent / row_total).astype(BF16)
        attn_blocks.append(
            jnp.einsum("hqk,khd->qhd", attn_probs, value_bf, preferred_element_type=F32)
        )
        log_totals.append(top_score[..., 0] + jnp.log(row_total[..., 0]))
    heads_out = jnp.concatenate(attn_blocks, axis=0).reshape(seq_len, local_width).astype(BF16)
    heads_out = after(heads_out, *near)
    attn_sum = scatter_halves(dot(heads_out, out_w).astype(BF16))
    hidden_res = residual_in + after(attn_sum, *far)
    normed_two, scale_two = norm_rows(hidden_res)
    second_in = (normed_two * moe_gain).astype(BF16)

    router_probs = jax.nn.softmax(dot_nt(second_in, router_w), axis=-1)
    own_routes = lax.dynamic_slice_in_dim(routes, tp_rank * piece, piece, 0)
    routed = jnp.any(
        own_routes[:, :, None] == jnp.arange(expert_count, dtype=jnp.int32)[None, None, :], axis=1
    ).astype(F32)
    gates = router_probs * routed
    gates_high = gates.astype(BF16)
    gates_low = (gates - gates_high.astype(F32)).astype(BF16)
    sent = jnp.concatenate(
        [
            second_in,
            gates_high,
            gates_low,
            jnp.zeros((piece, extra - 2 * expert_count), BF16),
        ],
        axis=1,
    )

    grad_around = lax.all_gather(jnp.stack(around), "tp", axis=1, tiled=True)
    grad_sets = [grad_own, grad_around, swap_core(grad_own), swap_core(grad_around)]
    down_grads = [
        dot_nt(one.reshape(-1, model_width), down_w).astype(BF16).reshape(-1, seq_len, hidden_all)
        for one in grad_sets
    ]
    sources = around_nodes(sent)
    owns = [gather_halves(sent)]
    for source in sources:
        owns.append(lax.all_gather(source, "tp", axis=0, tiled=True))
    defer = nodes <= 4
    by_hops = tp_count == 4
    kept, gate_dots, backs, swaps, hops, lasts, returns = (), [], [], [], [], [], []
    outs, outs_back = [], []
    base = jnp.reshape(fsdp_rank * local_experts, (1,)).astype(jnp.int32)

    def one_sequence(step, other, rows):
        nonlocal kept
        grads = down_grads[(1 if step > 0 else 0) + (2 if other else 0)]
        back, out, dots, kept = expert_products(
            base,
            rows,
            grads[max(step - 1, 0)],
            w_gate,
            w_up,
            w_down,
            2 * nodes,
            step + (nodes if other else 0),
            kept,
            expert_count,
        )
        return back, out, dots[:, :expert_count]

    def outputs_home(outs, steps):
        outs = jnp.stack([plus(own, swap_core(other)).astype(BF16) for own, other in outs])
        outs = lax.psum_scatter(outs, "tp", scatter_dimension=1, tiled=True)
        return [shift_node(outs[i], -step) for i, step in enumerate(steps)]

    for step in range(nodes):
        own = owns[step]
        other = swap_core(own)
        if by_hops and step > 1:
            own = after(own, *hops[step - 2][2])
            other = after(other, *lasts[step - 2])
        if step == 0:
            first = one_sequence(step, False, after(own, *sources))
            second = one_sequence(step, True, after(other, grad_around))
            mine, others = first, second
        else:
            if by_hops:
                own = after(own, *hops[step - 1][2])
            first = one_sequence(step, True, other)
            second = one_sequence(step, False, own)
            mine, others = second, first
        if step + 1 < nodes:
            owns[step + 1] = after(owns[step + 1], first[0])
        gate_dots.append((mine[2], others[2]))
        backs.append(mine[0])
        swaps.append(swap_core(others[0]))
        outs.append((mine[1], others[1]))
        if by_hops:
            hops.append(hop_one(mine[0], swaps[-1]))
            lasts.append(hop_two(*hops[-1]))
            returns.append(shift_node(hop_sum(*hops[-1], lasts[-1]).astype(BF16), -step))
        else:
            back_own = plus(mine[0], swaps[-1]).astype(BF16)
            total = lax.psum_scatter(back_own, "tp", scatter_dimension=0, tiled=True)
            returns.append(shift_node(total, -step))
        if not defer:
            outs_back += outputs_home(outs, [step])
            outs = []
            kept = after(kept, outs_back[-1], returns[-1])
    if defer:
        late = owns[-1]
        for steps in ([1, 2], [0, 3]) if nodes == 4 else [list(range(nodes))]:
            outs_back += outputs_home([after(outs[step], late) for step in steps], steps)
    hidden_kept, gate_kept, up_kept, rows_kept = kept

    def down_product(index, *earlier):
        grads = grad_sets[index].reshape(-1, model_width)
        start = (0, 1, nodes, nodes + 1)[index]
        count = grads.shape[0] // seq_len
        hidden = hidden_kept[start : start + count].reshape(-1, hidden_all)
        return dot_tn(after(hidden, *earlier), grads)

    down_w_grad = down_product(0) + down_product(1)
    pins = hops[-1][2] if by_hops else ()
    down_w_grad = down_w_grad + (down_product(2, *pins) + down_product(3, *pins))
    if by_hops and nodes > 1:
        returns[-1] = after(returns[-1], down_w_grad)

    def wide_product(grads, *earlier):
        rows = rows_kept.reshape(-1, model_width)
        grads = after(grads, *earlier).reshape(-1, hidden_all)
        return dot_tn(rows, grads).reshape(
            model_width, local_experts, hidden_slice
        ).transpose(1, 0, 2)

    back_sum = sum(one.astype(F32) for one in returns)
    output = (hidden_res + sum(one.astype(F32) for one in outs_back)).astype(BF16)

    node, core = fsdp_rank // 2, fsdp_rank % 2
    blocks = []
    for mine, others in gate_dots:
        blocks.append(
            jnp.where(core == 0, jnp.stack([mine.T, others.T], 1), jnp.stack([others.T, mine.T], 1))
        )
    blocks = jnp.stack(blocks[::-1] + blocks[::-1], axis=1)
    blocks = lax.dynamic_slice_in_dim(blocks, nodes - 1 - node, nodes, 1)
    prob_grad = lax.psum_scatter(
        blocks.reshape(expert_count, fsdp_count * seq_len),
        ("fsdp", "tp"),
        scatter_dimension=1,
        tiled=True,
    ).T

    grad_out = cotangent.astype(F32)
    prob_grad = prob_grad * routed
    logit_grad = router_probs * (
        prob_grad - jnp.sum(router_probs * prob_grad, axis=-1, keepdims=True)
    )
    router_grad = lax.dot_general(
        logit_grad,
        second_in.astype(F32),
        (((0,), (0,)), ((), ())),
        precision=lax.Precision.HIGHEST,
    )
    second_grad = back_sum + jnp.dot(
        logit_grad, router_w.astype(F32), precision=lax.Precision.HIGHEST
    )
    moe_gain_grad = jnp.sum(normed_two * second_grad, axis=0)
    residual_grad = grad_out + norm_back(normed_two, scale_two, second_grad * moe_gain)

    residual_all = gather_halves(residual_grad.astype(BF16))

    gate_w_grad = wide_product(gate_kept, *returns[1:])
    residual_all = after(residual_all, gate_w_grad)

    out_w_grad = dot_tn(heads_out, residual_all)
    heads_grad = dot_nt(residual_all, out_w).astype(BF16).reshape(head_shape)
    key_rot_grad = jnp.zeros(head_shape, F32)
    value_grad = jnp.zeros(head_shape, F32)
    query_blocks_grad = []
    for block_index in range(block_count):
        query_block, scores, causal = block_scores(block_index)
        log_block = log_totals[block_index]
        probs_full = jnp.where(causal[None], jnp.exp(scores - log_block[..., None]), 0.0)
        probs_bf = probs_full.astype(BF16)
        out_block = block_of(heads_grad, block_index)
        value_grad = value_grad + jnp.einsum(
            "hqk,qhd->khd", probs_bf, out_block, preferred_element_type=F32
        )
        prob_block_grad = jnp.einsum(
            "qhd,khd->hqk", out_block, value_bf, preferred_element_type=F32
        )
        centre = jnp.sum(probs_full * prob_block_grad, axis=-1, keepdims=True)
        score_grad = (probs_full * (prob_block_grad - centre)).astype(BF16)
        query_blocks_grad.append(
            jnp.einsum("hqk,khd->qhd", score_grad, key_bf, preferred_element_type=F32)
            * scale_factor
        )
        key_rot_grad = (
            key_rot_grad
            + jnp.einsum("hqk,qhd->khd", score_grad, query_block, preferred_element_type=F32)
            * scale_factor
        )
    query_rot_grad = jnp.concatenate(query_blocks_grad, axis=0)
    query_norm_grad = (query_rot_grad * cosine + rotate_back(query_rot_grad * sine_table)).reshape(
        seq_len, local_width
    )
    key_norm_grad = (key_rot_grad * cosine + rotate_back(key_rot_grad * sine_table)).reshape(
        seq_len, local_width
    )
    qgain_local = jnp.sum(query_raw * query_scale * query_norm_grad, axis=0)
    kgain_local = jnp.sum(key_raw * key_scale * key_norm_grad, axis=0)
    query_inner = query_norm_grad * local_qgain
    key_inner = key_norm_grad * local_kgain
    dots = sum_tp(
        jnp.stack(
            [jnp.sum(query_raw * query_inner, axis=-1), jnp.sum(key_raw * key_inner, axis=-1)]
        )
    )
    query_raw_grad = (
        query_scale * query_inner - query_raw * query_scale**3 * dots[0][:, None] / model_width
    ).astype(BF16)
    key_raw_grad = (
        key_scale * key_inner - key_raw * key_scale**3 * dots[1][:, None] / model_width
    ).astype(BF16)
    value_raw_grad = value_grad.reshape(seq_len, local_width).astype(BF16)
    qkv_grad = jnp.concatenate([query_raw_grad, key_raw_grad, value_raw_grad], axis=1)
    first_part = dot_nt(qkv_grad, qkv_w).astype(BF16)
    first_grad = scatter_halves(first_part)
    qkv_w_grad = dot_tn(first_all, qkv_grad).astype(BF16)
    up_w_grad = wide_product(up_kept, first_part, qkv_w_grad)
    down_w_grad = down_w_grad.reshape(local_experts, hidden_slice, model_width)

    attn_gain_grad = jnp.sum(normed_one * first_grad, axis=0)
    input_grad = residual_grad + norm_back(normed_one, scale_one, first_grad * attn_gain)

    def scatter_fsdp(grad, dimension):
        return lax.psum_scatter(
            grad.astype(BF16), "fsdp", scatter_dimension=dimension, tiled=True
        ).astype(F32)

    qkv_out = scatter_fsdp(qkv_w_grad, 0)
    out_w_out = scatter_fsdp(out_w_grad, 1)

    def widen(grad):
        return lax.dynamic_update_slice_in_dim(
            jnp.zeros((1, model_width), F32), grad[None], column_start, 1
        )

    early_out = reduce_small(jnp.concatenate([moe_gain_grad[None], router_grad], axis=0))
    late_out = reduce_small(
        jnp.concatenate(
            [attn_gain_grad[None], widen(qgain_local), widen(kgain_local)], axis=0
        )
    )
    return (
        output,
        input_grad,
        late_out[0],
        qkv_out[:, :local_width],
        qkv_out[:, local_width : 2 * local_width],
        qkv_out[:, 2 * local_width :],
        late_out[1],
        late_out[2],
        out_w_out,
        early_out[0],
        early_out[1:].T,
        gate_w_grad,
        up_w_grad,
        down_w_grad,
    )


def solution(mesh):
    placed = (
        P(("fsdp", "tp"), None),
        P(("fsdp", "tp"), None),
        P("fsdp", None),
        P("fsdp"),
        P("fsdp", "tp"),
        P("fsdp", "tp"),
        P("fsdp", "tp"),
        P("fsdp"),
        P("fsdp"),
        P("tp", "fsdp"),
        P("fsdp"),
        P("fsdp", None),
        P("fsdp", None, "tp"),
        P("fsdp", None, "tp"),
        P("fsdp", "tp", None),
    )
    return jax.shard_map(
        shards,
        mesh=mesh,
        in_specs=placed,
        out_specs=(
            P(("fsdp", "tp"), None),
            P(("fsdp", "tp"), None),
            P("fsdp"),
            P("fsdp", "tp"),
            P("fsdp", "tp"),
            P("fsdp", "tp"),
            P("fsdp"),
            P("fsdp"),
            P("tp", "fsdp"),
            P("fsdp"),
            P("fsdp", None),
            P("fsdp", None, "tp"),
            P("fsdp", None, "tp"),
            P("fsdp", "tp", None),
        ),
        check_vma=False,
    )
```

```python
import functools

import jax
import jax.numpy as jnp
from jax import lax
from jax.experimental import pallas as pl
from jax.experimental.pallas import tpu as pltpu
from jax.sharding import PartitionSpec as P

HEAD_DIM = 128
EPSILON = 1e-05
ROPE_BASE = 10000.0
F32 = jnp.float32
BF16 = jnp.bfloat16


def dot(a, b):
    return jnp.dot(a, b, preferred_element_type=F32)


def dot_nt(a, b):
    return lax.dot_general(a, b, (((1,), (1,)), ((), ())), preferred_element_type=F32)


def dot_tn(a, b):
    return lax.dot_general(a, b, (((0,), (0,)), ((), ())), preferred_element_type=F32)


def swap_core(operand):
    count = lax.axis_size("fsdp")
    return lax.ppermute(operand, "fsdp", [(i, i ^ 1) for i in range(count)])


def shift_node(operand, step):
    count = lax.axis_size("fsdp")
    nodes = count // 2
    if step % nodes == 0:
        return operand
    return lax.ppermute(
        operand, "fsdp", [(i, ((i // 2 + step) % nodes) * 2 + i % 2) for i in range(count)]
    )


def around_nodes(operand, *between):
    count = lax.axis_size("fsdp") // 2
    pieces = []
    for step in range(1, count - 1):
        pieces.append(shift_node(after(pieces[-1], *between) if pieces else operand, 1))
    if count > 1:
        pieces.append(shift_node(operand, -1))
    return pieces


def swap_tp(operand, mask):
    count = lax.axis_size("tp")
    return lax.ppermute(operand, "tp", [(i, i ^ mask) for i in range(count)])


def after(operand, *earlier):
    return lax.optimization_barrier((operand,) + earlier)[0]


def gather_halves(operand):
    if lax.axis_size("tp") != 4:
        return lax.all_gather(operand, "tp", axis=0, tiled=True)
    rows = operand.shape[0]
    half = rows // 2
    a, b = operand[:half], operand[half:]
    a1 = swap_tp(a, 1)
    b2 = swap_tp(b, 2)
    b1 = swap_tp(b, 1)
    a2 = swap_tp(a, 2)
    a3 = swap_tp(a1, 2)
    b3 = swap_tp(b2, 1)
    rank = lax.axis_index("tp")
    placed = jnp.zeros((4 * rows,) + operand.shape[1:], operand.dtype)
    for mask, part, offset in (
        (0, operand, 0),
        (1, a1, 0),
        (1, b1, half),
        (2, a2, 0),
        (2, b2, half),
        (3, a3, 0),
        (3, b3, half),
    ):
        placed = lax.dynamic_update_slice_in_dim(placed, part, (rank ^ mask) * rows + offset, 0)
    return placed


def plus(mine, other):
    return mine.astype(F32) + other.astype(F32)


def hop_one(operand, other=None):
    rows = operand.shape[0] // 4
    half = rows // 2
    rank = lax.axis_index("tp")

    def part(mask, offset):
        start = (rank ^ mask) * rows + offset
        mine = lax.dynamic_slice_in_dim(operand, start, half, 0)
        if other is None:
            return mine
        return plus(mine, lax.dynamic_slice_in_dim(other, start, half, 0))

    arrived = (
        swap_tp(part(3, 0).astype(BF16), 2),
        swap_tp(part(3, half).astype(BF16), 1),
        swap_tp(part(2, 0).astype(BF16), 2),
        swap_tp(part(1, half).astype(BF16), 1),
    )
    return part, half, arrived


def hop_two(part, half, arrived):
    a3, b3, _, _ = arrived
    return (
        swap_tp(plus(part(1, 0), a3).astype(BF16), 1),
        swap_tp(plus(part(2, half), b3).astype(BF16), 2),
    )


def hop_sum(part, half, arrived, last):
    _, _, a2, b1 = arrived
    ra = plus(plus(part(0, 0), a2), last[0])
    rb = plus(plus(part(0, half), b1), last[1])
    return jnp.concatenate([ra, rb], axis=0)


def scatter_halves(operand):
    if lax.axis_size("tp") != 4:
        return lax.psum_scatter(operand, "tp", scatter_dimension=0, tiled=True).astype(F32)
    first = hop_one(operand)
    return hop_sum(*first, hop_two(*first))


def scatter_dots(operand):
    if lax.axis_size("tp") != 4:
        return lax.psum_scatter(operand, "tp", scatter_dimension=2, tiled=True)
    rank = lax.axis_index("tp")
    size = operand.shape[2] // 4
    total = lax.dynamic_slice_in_dim(operand, rank * size, size, 2)
    for mask in (1, 2, 3):
        total = total + swap_tp(
            lax.dynamic_slice_in_dim(operand, (rank ^ mask) * size, size, 2), mask
        )
    return total


def gather_small(operand):
    count = lax.axis_size("fsdp")
    nodes = count // 2
    rank = lax.axis_index("fsdp")
    node, core = rank // 2, rank % 2
    other = swap_core(operand)
    pair = jnp.where(core == 0, jnp.stack([operand, other]), jnp.stack([other, operand]))
    around = [shift_node(pair, step) for step in range(nodes - 1, 0, -1)] + [pair]
    both = jnp.concatenate(around + around, axis=0)
    placed = lax.dynamic_slice_in_dim(both, 2 * (nodes - 1 - node), count, 0)
    return placed.transpose(1, 0, 2).reshape(operand.shape[0], -1)


def reduce_small(operand):
    count = lax.axis_size("fsdp")
    nodes = count // 2
    rank = lax.axis_index("fsdp")
    node, core = rank // 2, rank % 2
    blocks = operand.reshape(operand.shape[0], nodes, 2, -1).transpose(2, 1, 0, 3)
    mine = lax.dynamic_index_in_dim(blocks, core, 0, keepdims=False)
    mine = mine + swap_core(lax.dynamic_index_in_dim(blocks, 1 - core, 0, keepdims=False))
    total = lax.dynamic_index_in_dim(mine, node, 0, keepdims=False)
    for step in range(1, nodes):
        part = lax.dynamic_index_in_dim(mine, (node + step) % nodes, 0, keepdims=False)
        total = total + shift_node(part, step)
    return sum_tp(total)


def sum_tp(operand):
    if lax.axis_size("tp") != 4:
        return lax.psum(operand, "tp")
    return (operand + swap_tp(operand, 1)) + (swap_tp(operand, 2) + swap_tp(operand, 3))


def rope_tables(positions, columns):
    halfway = columns // 2
    frequency = ROPE_BASE ** (-2.0 * jnp.arange(halfway).astype(F32) / columns)
    angles = positions.astype(F32)[:, None] * frequency[None, :]
    angles = jnp.concatenate([angles, angles], axis=-1)
    return (jnp.cos(angles)[:, None, :], jnp.sin(angles)[:, None, :])


def rotate(tensor):
    halfway = tensor.shape[-1] // 2
    return jnp.concatenate([-tensor[..., halfway:], tensor[..., :halfway]], axis=-1)


def rotate_back(tensor):
    halfway = tensor.shape[-1] // 2
    return jnp.concatenate([tensor[..., halfway:], -tensor[..., :halfway]], axis=-1)


def norm_rows(tensor):
    row_scale = lax.rsqrt(jnp.mean(tensor * tensor, axis=-1, keepdims=True) + EPSILON)
    return (tensor * row_scale, row_scale)


def norm_back(normed, row_scale, grad_normed):
    return row_scale * (
        grad_normed - normed * jnp.mean(normed * grad_normed, axis=-1, keepdims=True)
    )


def expert_kernel(extra, experts, base, *refs):
    x_ref, z_ref, gate_w, up_w, down_w = refs[:5]
    back_ref, out_ref, dots_ref, hidden_ref, gate_grad_ref, up_grad_ref, copy_ref = refs[-8:-1]
    gated_ref = refs[-1]
    count, width, size = gate_w.shape
    x = x_ref[:, :width]
    copy_ref[0] = x.T
    ends = x_ref[:, width:].astype(F32)
    lane = lax.broadcasted_iota(jnp.int32, ends.shape, 1)
    dots = jnp.zeros(ends.shape, F32)
    for e in range(count):
        columns = slice(e * size, (e + 1) * size)
        number = base[0] + e
        gate = jnp.sum(
            jnp.where((lane == number) | (lane == number + experts), ends, 0.0),
            axis=1,
            keepdims=True,
        )
        gate_pre = dot(x, gate_w[e])
        up_pre = dot(x, up_w[e])
        down_grad = z_ref[:, columns].astype(F32)
        sigmoid_gate = 1.0 / (1.0 + jnp.exp(-gate_pre))
        activated = gate_pre * sigmoid_gate
        hidden = activated * up_pre
        gated = (hidden * gate).astype(BF16)
        gated_ref[:, columns] = gated
        hidden_ref[0, columns, :] = gated.T
        dots = dots + jnp.where(
            lane == e, jnp.sum(hidden * down_grad, axis=1, keepdims=True), 0.0
        )
        hidden_grad = down_grad * gate
        gate_grad_ref[0, :, columns] = (
            hidden_grad * up_pre * sigmoid_gate * (1.0 + gate_pre * (1.0 - sigmoid_gate))
        ).astype(BF16)
        up_grad_ref[0, :, columns] = (hidden_grad * activated).astype(BF16)
    dots_ref[...] = dots
    tile = min(512, width)
    for start in range(0, width, tile):
        rows = slice(start, start + tile)
        back = jnp.zeros((x.shape[0], tile), F32)
        out = jnp.zeros((x.shape[0], tile), F32)
        for e in range(count):
            columns = slice(e * size, (e + 1) * size)
            back = back + dot_nt(gate_grad_ref[0, :, columns], gate_w[e, rows, :])
            back = back + dot_nt(up_grad_ref[0, :, columns], up_w[e, rows, :])
            out = out + dot(gated_ref[:, columns], down_w[e, :, rows])
        back_ref[:, rows] = back.astype(BF16)
        out_ref[:, rows] = out.astype(BF16)


def expert_products(base, x, z, gate_w, up_w, down_w, slots, slot, kept, experts):
    rows, wide = x.shape
    count, width, size = gate_w.shape
    extra = wide - width
    block = min(256, rows)
    hidden = count * size

    def whole(array):
        return pl.BlockSpec(
            array.shape, lambda i, base: (0, 0, 0), pipeline_mode=pl.Buffered(1)
        )

    def by_rows(columns):
        return pl.BlockSpec((block, columns), lambda i, base: (i, 0))

    def in_slot(columns):
        return pl.BlockSpec((1, block, columns), lambda i, base: (slot, i, 0))

    def turned_in_slot(columns):
        return pl.BlockSpec((1, columns, block), lambda i, base: (slot, 0, i))

    kept_shapes = [
        jax.ShapeDtypeStruct((slots, hidden, rows), BF16),
        jax.ShapeDtypeStruct((slots, rows, hidden), BF16),
        jax.ShapeDtypeStruct((slots, rows, hidden), BF16),
        jax.ShapeDtypeStruct((slots, width, rows), BF16),
    ]
    results = pl.pallas_call(
        functools.partial(expert_kernel, extra, experts),
        out_shape=[
            jax.ShapeDtypeStruct((rows, width), BF16),
            jax.ShapeDtypeStruct((rows, width), BF16),
            jax.ShapeDtypeStruct((rows, extra), F32),
        ]
        + kept_shapes,
        grid_spec=pltpu.PrefetchScalarGridSpec(
            num_scalar_prefetch=1,
            grid=(rows // block,),
            in_specs=[by_rows(wide), by_rows(hidden), whole(gate_w), whole(up_w), whole(down_w)]
            + [pl.BlockSpec(memory_space=pl.ANY)] * len(kept),
            out_specs=[by_rows(width), by_rows(width), by_rows(extra)]
            + [turned_in_slot(hidden), in_slot(hidden), in_slot(hidden), turned_in_slot(width)],
            scratch_shapes=[pltpu.VMEM((block, hidden), BF16)],
        ),
        input_output_aliases={6 + i: 3 + i for i in range(len(kept))},
        cost_estimate=pl.CostEstimate(
            flops=10 * rows * width * hidden,
            bytes_accessed=6 * width * hidden + 2 * rows * (4 * width + 4 * hidden),
            transcendentals=rows * hidden,
        ),
        compiler_params=pltpu.CompilerParams(vmem_limit_bytes=60 * 1024 * 1024),
    )(base, x, z, gate_w, up_w, down_w, *kept)
    return results[0], results[1], results[2], tuple(results[3:])


def wide_kernel(left, right, out_ref):
    count, width, size = out_ref.shape
    tile = min(512, width)
    for start in range(0, width, tile):
        rows = slice(start, start + tile)
        part = dot(left[0, rows, :], right[0])

        @pl.when(pl.program_id(0) == 0)
        def _():
            for e in range(count):
                out_ref[e, rows, :] = part[:, e * size : (e + 1) * size]

        @pl.when(pl.program_id(0) > 0)
        def _():
            for e in range(count):
                out_ref[e, rows, :] += part[:, e * size : (e + 1) * size]


def wide_products(turned, grads, count):
    slots, width, rows = turned.shape
    hidden = grads.shape[2]
    size = hidden // count
    return pl.pallas_call(
        wide_kernel,
        out_shape=jax.ShapeDtypeStruct((count, width, size), F32),
        grid=(slots,),
        in_specs=[
            pl.BlockSpec((1, width, rows), lambda k: (k, 0, 0)),
            pl.BlockSpec((1, rows, hidden), lambda k: (k, 0, 0)),
        ],
        out_specs=pl.BlockSpec((count, width, size), lambda k: (0, 0, 0)),
        cost_estimate=pl.CostEstimate(
            flops=2 * slots * rows * width * hidden,
            bytes_accessed=2 * slots * rows * (width + hidden) + 4 * width * hidden,
            transcendentals=0,
        ),
        compiler_params=pltpu.CompilerParams(vmem_limit_bytes=60 * 1024 * 1024),
    )(turned, grads)


def down_kernel(has_first, left, near, far, *refs):
    out_ref = refs[-1]
    step = pl.program_id(0)
    height, width = out_ref.shape
    tile = min(512, width)

    @pl.when(step == 0)
    def _():
        for start in range(0, width, tile):
            columns = slice(start, start + tile)
            part = dot(left[0], near[0, :, columns])
            if has_first:
                part = part + refs[0][:, columns]
            out_ref[:, columns] = part

    @pl.when(step > 0)
    def _():
        for start in range(0, width, tile):
            columns = slice(start, start + tile)
            out_ref[:, columns] += dot(left[0], far[0, :, columns])


def down_products(turned, slot, near, far, first=None):
    _, hidden, rows = turned.shape
    width = near.shape[1]
    count = far.shape[0]
    constant = pl.BlockSpec(
        (hidden, width), lambda k: (0, 0), pipeline_mode=pl.Buffered(1)
    )
    return pl.pallas_call(
        functools.partial(down_kernel, first is not None),
        out_shape=jax.ShapeDtypeStruct((hidden, width), F32),
        grid=(count + 1,),
        in_specs=[
            pl.BlockSpec((1, hidden, rows), lambda k: (slot + k, 0, 0)),
            pl.BlockSpec((1, rows, width), lambda k: (0, 0, 0), pipeline_mode=pl.Buffered(1)),
            pl.BlockSpec((1, rows, width), lambda k: (jnp.maximum(k - 1, 0), 0, 0)),
        ]
        + ([constant] if first is not None else []),
        out_specs=pl.BlockSpec((hidden, width), lambda k: (0, 0)),
        cost_estimate=pl.CostEstimate(
            flops=2 * (count + 1) * rows * width * hidden,
            bytes_accessed=2 * (count + 1) * rows * (width + hidden) + 4 * width * hidden,
            transcendentals=0,
        ),
        compiler_params=pltpu.CompilerParams(vmem_limit_bytes=60 * 1024 * 1024),
    )(turned, near[None], far, *(() if first is None else (first,)))


def swap_rows(grad):
    count = lax.axis_size("fsdp")
    core = lax.axis_index("fsdp") % 2
    blocks = grad.reshape(count // 2, 2, grad.shape[0] // count, grad.shape[1])
    return (
        lax.dynamic_index_in_dim(blocks, core, 1, keepdims=False),
        swap_core(lax.dynamic_index_in_dim(blocks, 1 - core, 1, keepdims=False)),
    )


def sum_rows(mine, arrived):
    nodes = mine.shape[0]
    node = lax.axis_index("fsdp") // 2

    def part(step):
        place = (node + step) % nodes
        return plus(
            lax.dynamic_index_in_dim(mine, place, 0, keepdims=False),
            lax.dynamic_index_in_dim(arrived, place, 0, keepdims=False),
        )

    total = part(0)
    for step in range(1, nodes):
        total = total + shift_node(part(step).astype(BF16), step).astype(F32)
    return total


def shards(
    tokens,
    cotangent,
    routes,
    gain_attn,
    w_query,
    w_key,
    w_value,
    gain_query,
    gain_key,
    w_out,
    gain_moe,
    w_router,
    w_gate,
    w_up,
    w_down,
):
    tp_count = lax.axis_size("tp")
    tp_rank = lax.axis_index("tp")
    fsdp_count = lax.axis_size("fsdp")
    fsdp_rank = lax.axis_index("fsdp")
    nodes = fsdp_count // 2
    piece, model_width = tokens.shape
    seq_len = piece * tp_count
    local_width = w_query.shape[1]
    head_count = local_width // HEAD_DIM
    expert_count = w_router.shape[1]
    local_experts, _, hidden_slice = w_gate.shape
    hidden_all = local_experts * hidden_slice
    extra = -(-2 * expert_count // 128) * 128
    scale_factor = HEAD_DIM ** (-0.5)
    head_shape = (seq_len, head_count, HEAD_DIM)
    column_start = tp_rank * local_width

    small = gather_small(
        jnp.concatenate(
            [gain_attn[None], gain_moe[None], gain_query[None], gain_key[None], w_router.T], axis=0
        )
    )
    attn_gain, moe_gain = small[0].astype(F32), small[1].astype(F32)
    local_gains = lax.dynamic_slice_in_dim(small[2:4], column_start, local_width, 1).astype(F32)
    local_qgain, local_kgain = local_gains[0], local_gains[1]
    router_w = small[4:]
    qkv_w = lax.all_gather(
        jnp.concatenate([w_query, w_key, w_value], axis=1), "fsdp", axis=0, tiled=True
    )
    out_w = lax.all_gather(w_out, "fsdp", axis=1, tiled=True)

    down_w = w_down.reshape(hidden_all, model_width)

    residual_in = tokens.astype(F32)
    normed_one, scale_one = norm_rows(residual_in)
    first_in = (normed_one * attn_gain).astype(BF16)
    first_all = gather_halves(first_in)

    early = after(cotangent, qkv_w, first_all)
    grad_own = lax.all_gather(early, "tp", axis=0, tiled=True)
    qkv_raw = dot(first_all, qkv_w)
    around = around_nodes(early, qkv_raw)
    query_raw = qkv_raw[:, :local_width]
    key_raw = qkv_raw[:, local_width : 2 * local_width]
    value_raw = qkv_raw[:, 2 * local_width :]
    squares = sum_tp(
        jnp.stack([jnp.sum(query_raw * query_raw, axis=-1), jnp.sum(key_raw * key_raw, axis=-1)])
    )
    query_scale = lax.rsqrt(squares[0] / model_width + EPSILON)[:, None]
    key_scale = lax.rsqrt(squares[1] / model_width + EPSILON)[:, None]
    positions = jnp.arange(seq_len, dtype=jnp.int32)
    cosine, sine_table = rope_tables(positions, HEAD_DIM)
    query_normed = (query_raw * query_scale * local_qgain).reshape(head_shape)
    key_normed = (key_raw * key_scale * local_kgain).reshape(head_shape)
    query_bf = (query_normed * cosine + rotate(query_normed) * sine_table).astype(BF16)
    key_bf = (key_normed * cosine + rotate(key_normed) * sine_table).astype(BF16)
    value_bf = value_raw.astype(BF16).reshape(head_shape)
    block_rows = min(512, seq_len)
    block_count = seq_len // block_rows

    def block_of(array, block_index):
        return array[block_index * block_rows : (block_index + 1) * block_rows]

    def block_scores(block_index):
        query_block = block_of(query_bf, block_index)
        scores = (
            jnp.einsum("qhd,khd->hqk", query_block, key_bf, preferred_element_type=F32)
            * scale_factor
        )
        causal = block_of(positions, block_index)[:, None] >= positions[None, :]
        return (query_block, jnp.where(causal[None], scores, -1e30), causal)

    attn_blocks, log_totals = [], []
    for block_index in range(block_count):
        query_block, scores, causal = block_scores(block_index)
        top_score = jnp.max(scores, axis=-1, keepdims=True)
        exponent = jnp.exp(scores - top_score)
        row_total = jnp.sum(exponent, axis=-1, keepdims=True)
        attn_probs = (exponent / row_total).astype(BF16)
        attn_blocks.append(
            jnp.einsum("hqk,khd->qhd", attn_probs, value_bf, preferred_element_type=F32)
        )
        log_totals.append(top_score[..., 0] + jnp.log(row_total[..., 0]))
    heads_out = jnp.concatenate(attn_blocks, axis=0).reshape(seq_len, local_width).astype(BF16)
    heads_out = after(heads_out, grad_own)
    attn_sum = scatter_halves(dot(heads_out, out_w).astype(BF16))
    hidden_res = residual_in + attn_sum
    normed_two, scale_two = norm_rows(hidden_res)
    second_in = (normed_two * moe_gain).astype(BF16)

    router_probs = jax.nn.softmax(dot_nt(second_in, router_w), axis=-1)
    own_routes = lax.dynamic_slice_in_dim(routes, tp_rank * piece, piece, 0)
    routed = jnp.any(
        own_routes[:, :, None] == jnp.arange(expert_count, dtype=jnp.int32)[None, None, :], axis=1
    ).astype(F32)
    gates = router_probs * routed
    gates_high = gates.astype(BF16)
    gates_low = (gates - gates_high.astype(F32)).astype(BF16)
    sent = jnp.concatenate(
        [
            second_in,
            gates_high,
            gates_low,
            jnp.zeros((piece, extra - 2 * expert_count), BF16),
        ],
        axis=1,
    )

    grad_around = lax.all_gather(
        after(jnp.stack(around), attn_blocks[0]), "tp", axis=1, tiled=True
    )
    grad_sets = [grad_own, grad_around, swap_core(grad_own), swap_core(grad_around)]
    down_grads = [
        dot_nt(one.reshape(-1, model_width), down_w).astype(BF16).reshape(-1, seq_len, hidden_all)
        for one in grad_sets
    ]
    sources = around_nodes(sent)
    owns = [gather_halves(sent)]
    for source in sources:
        owns.append(lax.all_gather(source, "tp", axis=0, tiled=True))
    defer = nodes <= 4
    by_hops = tp_count == 4
    kept, gate_dots, backs, swaps, hops, lasts, returns = (), [], [], [], [], [], []
    outs, outs_back, wholes = [], [], []
    base = jnp.reshape(fsdp_rank * local_experts, (1,)).astype(jnp.int32)

    def one_sequence(step, other, rows):
        nonlocal kept
        grads = down_grads[(1 if step > 0 else 0) + (2 if other else 0)]
        back, out, dots, kept = expert_products(
            base,
            rows,
            grads[max(step - 1, 0)],
            w_gate,
            w_up,
            w_down,
            2 * nodes,
            step + (nodes if other else 0),
            kept,
            expert_count,
        )
        return back, out, dots[:, :local_experts].T

    def outputs_home(out, step):
        whole = plus(out[0], swap_core(out[1])).astype(BF16)
        wholes.append(whole)
        return [lax.psum_scatter(whole, "tp", scatter_dimension=0, tiled=True)]

    for step in range(nodes):
        own = owns[step]
        other = swap_core(own)
        if by_hops and step > 1:
            own = after(own, *hops[step - 2][2])
            other = after(other, *lasts[step - 2])
        if step == 0:
            first = one_sequence(step, False, after(own, *sources))
            second = one_sequence(step, True, after(other, grad_around))
            mine, others = first, second
        else:
            if by_hops:
                own = after(own, *hops[step - 1][2])
            first = one_sequence(step, True, other)
            second = one_sequence(step, False, own)
            mine, others = second, first
        if step + 1 < nodes:
            owns[step + 1] = after(owns[step + 1], first[0])
        gate_dots.append((mine[2], others[2]))
        backs.append(mine[0])
        swaps.append(swap_core(others[0]))
        outs.append((mine[1], others[1]))
        if by_hops:
            hops.append(hop_one(mine[0], swaps[-1]))
            lasts.append(hop_two(*hops[-1]))
            returns.append(shift_node(hop_sum(*hops[-1], lasts[-1]).astype(BF16), -step))
        else:
            back_own = plus(mine[0], swaps[-1]).astype(BF16)
            total = lax.psum_scatter(back_own, "tp", scatter_dimension=0, tiled=True)
            returns.append(shift_node(total, -step))
        if not defer:
            outs_back += [shift_node(outputs_home(outs[step], step)[0], -step)]
            kept = after(kept, outs_back[-1], returns[-1])
    if defer:
        late = owns[-1]
        for step in range(nodes):
            outs_back += outputs_home(after(outs[step], late), step)
    hidden_kept, gate_kept, up_kept, rows_kept = kept

    down_w_grad = down_products(hidden_kept, 0, grad_own, grad_around)
    pins = hops[-1][2] if by_hops else ()
    down_w_grad = down_products(
        after(hidden_kept, *pins), nodes, grad_sets[2], grad_sets[3], down_w_grad
    )
    if by_hops and nodes > 1:
        returns[-1] = after(returns[-1], down_w_grad)

    back_sum = sum(one.astype(F32) for one in returns)

    def home(step, *earlier):
        if defer:
            outs_back[step] = shift_node(after(outs_back[step], *earlier), -step)

    node, core = fsdp_rank // 2, fsdp_rank % 2
    dots = jnp.stack([one[0] for one in gate_dots] + [one[1] for one in gate_dots], axis=1)
    dots = scatter_dots(dots)
    mine, others = dots[:, :nodes], swap_core(dots[:, nodes:])
    pair = jnp.where(core == 0, jnp.stack([mine, others]), jnp.stack([others, mine]))
    placed = jnp.stack(
        [pair[:, :, 0]] + [shift_node(pair[:, :, step], -step) for step in range(1, nodes)]
    )
    placed = lax.dynamic_slice_in_dim(
        jnp.concatenate([placed, placed], axis=0), nodes - node, nodes, 0
    )
    prob_grad = placed.reshape(expert_count, piece).T

    grad_out = cotangent.astype(F32)
    prob_grad = prob_grad * routed
    logit_grad = router_probs * (
        prob_grad - jnp.sum(router_probs * prob_grad, axis=-1, keepdims=True)
    )
    router_grad = lax.dot_general(
        logit_grad,
        second_in.astype(F32),
        (((0,), (0,)), ((), ())),
        precision=lax.Precision.HIGHEST,
    )
    second_grad = back_sum + jnp.dot(
        logit_grad, router_w.astype(F32), precision=lax.Precision.HIGHEST
    )
    moe_gain_grad = jnp.sum(normed_two * second_grad, axis=0)
    residual_grad = grad_out + norm_back(normed_two, scale_two, second_grad * moe_gain)

    residual_all = gather_halves(residual_grad.astype(BF16))

    gate_w_grad = wide_products(rows_kept, after(gate_kept, *returns[1:], *wholes), local_experts)
    residual_all = after(residual_all, gate_w_grad)

    out_w_swapped = swap_rows(dot_tn(residual_all, heads_out).astype(BF16))
    out_w_out = sum_rows(*out_w_swapped).T
    early_out = reduce_small(jnp.concatenate([moe_gain_grad[None], router_grad], axis=0))
    heads_grad = dot_nt(residual_all, out_w).astype(BF16).reshape(head_shape)
    if nodes > 1:
        home(1, heads_grad)
    key_rot_grad = jnp.zeros(head_shape, F32)
    value_grad = jnp.zeros(head_shape, F32)
    query_blocks_grad = []
    for block_index in range(block_count):
        query_block, scores, causal = block_scores(block_index)
        log_block = log_totals[block_index]
        probs_full = jnp.where(causal[None], jnp.exp(scores - log_block[..., None]), 0.0)
        probs_bf = probs_full.astype(BF16)
        out_block = block_of(heads_grad, block_index)
        if block_index > 0:
            out_block = after(out_block, early_out, out_w_swapped[1], *outs_back[1:2])
            if block_index == 1 and nodes > 2:
                home(2, query_blocks_grad[0])
        value_grad = value_grad + jnp.einsum(
            "hqk,qhd->khd", probs_bf, out_block, preferred_element_type=F32
        )
        prob_block_grad = jnp.einsum(
            "qhd,khd->hqk", out_block, value_bf, preferred_element_type=F32
        )
        centre = jnp.sum(probs_full * prob_block_grad, axis=-1, keepdims=True)
        score_grad = (probs_full * (prob_block_grad - centre)).astype(BF16)
        query_blocks_grad.append(
            jnp.einsum("hqk,khd->qhd", score_grad, key_bf, preferred_element_type=F32)
            * scale_factor
        )
        key_rot_grad = (
            key_rot_grad
            + jnp.einsum("hqk,qhd->khd", score_grad, query_block, preferred_element_type=F32)
            * scale_factor
        )
    query_rot_grad = jnp.concatenate(query_blocks_grad, axis=0)
    query_norm_grad = (query_rot_grad * cosine + rotate_back(query_rot_grad * sine_table)).reshape(
        seq_len, local_width
    )
    key_norm_grad = (key_rot_grad * cosine + rotate_back(key_rot_grad * sine_table)).reshape(
        seq_len, local_width
    )
    qgain_local = jnp.sum(query_raw * query_scale * query_norm_grad, axis=0)
    kgain_local = jnp.sum(key_raw * key_scale * key_norm_grad, axis=0)
    query_inner = query_norm_grad * local_qgain
    key_inner = key_norm_grad * local_kgain
    dots = sum_tp(
        jnp.stack(
            [jnp.sum(query_raw * query_inner, axis=-1), jnp.sum(key_raw * key_inner, axis=-1)]
        )
    )
    query_raw_grad = (
        query_scale * query_inner - query_raw * query_scale**3 * dots[0][:, None] / model_width
    ).astype(BF16)
    key_raw_grad = (
        key_scale * key_inner - key_raw * key_scale**3 * dots[1][:, None] / model_width
    ).astype(BF16)
    value_raw_grad = value_grad.reshape(seq_len, local_width).astype(BF16)
    qkv_grad = jnp.concatenate([query_raw_grad, key_raw_grad, value_raw_grad], axis=1)
    qkv_grad = after(qkv_grad, out_w_out, *(outs_back[2:3] if block_count > 1 else []))
    first_part = dot_nt(qkv_grad, qkv_w).astype(BF16)
    first_grad = scatter_halves(first_part)
    home(0, first_part)
    for step in range(3 if block_count > 1 else 2, nodes):
        home(step, first_part)
    output = (hidden_res + sum(one.astype(F32) for one in outs_back)).astype(BF16)
    qkv_w_grad = dot_tn(first_all, qkv_grad).astype(BF16)
    up_w_grad = wide_products(rows_kept, after(up_kept, first_part, qkv_w_grad, outs_back[0], outs_back[-1]), local_experts)
    down_w_grad = down_w_grad.reshape(local_experts, hidden_slice, model_width)

    attn_gain_grad = jnp.sum(normed_one * first_grad, axis=0)
    input_grad = residual_grad + norm_back(normed_one, scale_one, first_grad * attn_gain)

    qkv_out = sum_rows(*swap_rows(qkv_w_grad))

    def widen(grad):
        return lax.dynamic_update_slice_in_dim(
            jnp.zeros((1, model_width), F32), grad[None], column_start, 1
        )

    late_out = reduce_small(
        jnp.concatenate(
            [attn_gain_grad[None], widen(qgain_local), widen(kgain_local)], axis=0
        )
    )
    return (
        output,
        input_grad,
        late_out[0],
        qkv_out[:, :local_width],
        qkv_out[:, local_width : 2 * local_width],
        qkv_out[:, 2 * local_width :],
        late_out[1],
        late_out[2],
        out_w_out,
        early_out[0],
        early_out[1:].T,
        gate_w_grad,
        up_w_grad,
        down_w_grad,
    )


def solution(mesh):
    placed = (
        P(("fsdp", "tp"), None),
        P(("fsdp", "tp"), None),
        P("fsdp", None),
        P("fsdp"),
        P("fsdp", "tp"),
        P("fsdp", "tp"),
        P("fsdp", "tp"),
        P("fsdp"),
        P("fsdp"),
        P("tp", "fsdp"),
        P("fsdp"),
        P("fsdp", None),
        P("fsdp", None, "tp"),
        P("fsdp", None, "tp"),
        P("fsdp", "tp", None),
    )
    return jax.shard_map(
        shards,
        mesh=mesh,
        in_specs=placed,
        out_specs=(
            P(("fsdp", "tp"), None),
            P(("fsdp", "tp"), None),
            P("fsdp"),
            P("fsdp", "tp"),
            P("fsdp", "tp"),
            P("fsdp", "tp"),
            P("fsdp"),
            P("fsdp"),
            P("tp", "fsdp"),
            P("fsdp"),
            P("fsdp", None),
            P("fsdp", None, "tp"),
            P("fsdp", None, "tp"),
            P("fsdp", "tp", None),
        ),
        check_vma=False,
    )
```

```python
import functools

import jax
import jax.numpy as jnp
from jax import lax
from jax.experimental import pallas as pl
from jax.experimental.pallas import tpu as pltpu
from jax.sharding import PartitionSpec as P

HEAD_DIM = 128
EPSILON = 1e-05
ROPE_BASE = 10000.0
F32 = jnp.float32
BF16 = jnp.bfloat16


def dot(a, b):
    return jnp.dot(a, b, preferred_element_type=F32)


def dot_nt(a, b):
    return lax.dot_general(a, b, (((1,), (1,)), ((), ())), preferred_element_type=F32)


def dot_tn(a, b):
    return lax.dot_general(a, b, (((0,), (0,)), ((), ())), preferred_element_type=F32)


def swap_core(operand):
    count = lax.axis_size("fsdp")
    return lax.ppermute(operand, "fsdp", [(i, i ^ 1) for i in range(count)])


def shift_node(operand, step):
    count = lax.axis_size("fsdp")
    nodes = count // 2
    if step % nodes == 0:
        return operand
    return lax.ppermute(
        operand, "fsdp", [(i, ((i // 2 + step) % nodes) * 2 + i % 2) for i in range(count)]
    )


def around_nodes(operand, *between):
    count = lax.axis_size("fsdp") // 2
    pieces = []
    for step in range(1, count - 1):
        pieces.append(shift_node(after(pieces[-1], *between) if pieces else operand, 1))
    if count > 1:
        pieces.append(shift_node(operand, -1))
    return pieces


def swap_tp(operand, mask):
    count = lax.axis_size("tp")
    return lax.ppermute(operand, "tp", [(i, i ^ mask) for i in range(count)])


def after(operand, *earlier):
    return lax.optimization_barrier((operand,) + earlier)[0]


def gather_halves(operand):
    if lax.axis_size("tp") != 4:
        return lax.all_gather(operand, "tp", axis=0, tiled=True)
    rows = operand.shape[0]
    half = rows // 2
    a, b = operand[:half], operand[half:]
    a1 = swap_tp(a, 1)
    b2 = swap_tp(b, 2)
    b1 = swap_tp(b, 1)
    a2 = swap_tp(a, 2)
    a3 = swap_tp(a1, 2)
    b3 = swap_tp(b2, 1)
    rank = lax.axis_index("tp")
    placed = jnp.zeros((4 * rows,) + operand.shape[1:], operand.dtype)
    for mask, part, offset in (
        (0, operand, 0),
        (1, a1, 0),
        (1, b1, half),
        (2, a2, 0),
        (2, b2, half),
        (3, a3, 0),
        (3, b3, half),
    ):
        placed = lax.dynamic_update_slice_in_dim(placed, part, (rank ^ mask) * rows + offset, 0)
    return placed


def gather_pieces(operand):
    if lax.axis_size("tp") != 4:
        return lax.all_gather(operand, "tp", axis=0, tiled=True)
    one = swap_tp(operand, 1)
    two = swap_tp(operand, 2)
    three = swap_tp(one, 2)
    rank = lax.axis_index("tp")
    placed = jnp.zeros((4,) + operand.shape, operand.dtype)
    for mask, part in enumerate((operand, one, two, three)):
        placed = lax.dynamic_update_slice_in_dim(placed, part[None], rank ^ mask, 0)
    return placed.reshape(-1, operand.shape[1])


def plus(mine, other):
    return mine.astype(F32) + other.astype(F32)


def hop_one(operand, other=None):
    rows = operand.shape[0] // 4
    half = rows // 2
    rank = lax.axis_index("tp")

    def part(mask, offset):
        start = (rank ^ mask) * rows + offset
        mine = lax.dynamic_slice_in_dim(operand, start, half, 0)
        if other is None:
            return mine
        return plus(mine, lax.dynamic_slice_in_dim(other, start, half, 0))

    arrived = (
        swap_tp(part(3, 0).astype(BF16), 2),
        swap_tp(part(3, half).astype(BF16), 1),
        swap_tp(part(2, 0).astype(BF16), 2),
        swap_tp(part(1, half).astype(BF16), 1),
    )
    return part, half, arrived


def hop_two(part, half, arrived):
    a3, b3, _, _ = arrived
    return (
        swap_tp(plus(part(1, 0), a3).astype(BF16), 1),
        swap_tp(plus(part(2, half), b3).astype(BF16), 2),
    )


def hop_sum(part, half, arrived, last):
    _, _, a2, b1 = arrived
    ra = plus(plus(part(0, 0), a2), last[0])
    rb = plus(plus(part(0, half), b1), last[1])
    return jnp.concatenate([ra, rb], axis=0)


def scatter_halves(operand):
    if lax.axis_size("tp") != 4:
        return lax.psum_scatter(operand, "tp", scatter_dimension=0, tiled=True).astype(F32)
    first = hop_one(operand)
    return hop_sum(*first, hop_two(*first))


def scatter_dots(operand):
    if lax.axis_size("tp") != 4:
        return lax.psum_scatter(operand, "tp", scatter_dimension=2, tiled=True)
    rank = lax.axis_index("tp")
    size = operand.shape[2] // 4
    total = lax.dynamic_slice_in_dim(operand, rank * size, size, 2)
    for mask in (1, 2, 3):
        total = total + swap_tp(
            lax.dynamic_slice_in_dim(operand, (rank ^ mask) * size, size, 2), mask
        )
    return total


def gather_small(operand):
    count = lax.axis_size("fsdp")
    nodes = count // 2
    rank = lax.axis_index("fsdp")
    node, core = rank // 2, rank % 2
    other = swap_core(operand)
    pair = jnp.where(core == 0, jnp.stack([operand, other]), jnp.stack([other, operand]))
    around = [shift_node(pair, step) for step in range(nodes - 1, 0, -1)] + [pair]
    both = jnp.concatenate(around + around, axis=0)
    placed = lax.dynamic_slice_in_dim(both, 2 * (nodes - 1 - node), count, 0)
    return placed.transpose(1, 0, 2).reshape(operand.shape[0], -1)


def reduce_small(operand):
    count = lax.axis_size("fsdp")
    nodes = count // 2
    rank = lax.axis_index("fsdp")
    node, core = rank // 2, rank % 2
    blocks = operand.reshape(operand.shape[0], nodes, 2, -1).transpose(2, 1, 0, 3)
    mine = lax.dynamic_index_in_dim(blocks, core, 0, keepdims=False)
    mine = mine + swap_core(lax.dynamic_index_in_dim(blocks, 1 - core, 0, keepdims=False))
    total = lax.dynamic_index_in_dim(mine, node, 0, keepdims=False)
    for step in range(1, nodes):
        part = lax.dynamic_index_in_dim(mine, (node + step) % nodes, 0, keepdims=False)
        total = total + shift_node(part, step)
    return sum_tp(total)


def sum_tp(operand):
    if lax.axis_size("tp") != 4:
        return lax.psum(operand, "tp")
    return (operand + swap_tp(operand, 1)) + (swap_tp(operand, 2) + swap_tp(operand, 3))


def rope_tables(positions, columns):
    halfway = columns // 2
    frequency = ROPE_BASE ** (-2.0 * jnp.arange(halfway).astype(F32) / columns)
    angles = positions.astype(F32)[:, None] * frequency[None, :]
    angles = jnp.concatenate([angles, angles], axis=-1)
    return (jnp.cos(angles)[:, None, :], jnp.sin(angles)[:, None, :])


def rotate(tensor):
    halfway = tensor.shape[-1] // 2
    return jnp.concatenate([-tensor[..., halfway:], tensor[..., :halfway]], axis=-1)


def rotate_back(tensor):
    halfway = tensor.shape[-1] // 2
    return jnp.concatenate([tensor[..., halfway:], -tensor[..., :halfway]], axis=-1)


def norm_rows(tensor):
    row_scale = lax.rsqrt(jnp.mean(tensor * tensor, axis=-1, keepdims=True) + EPSILON)
    return (tensor * row_scale, row_scale)


def norm_back(normed, row_scale, grad_normed):
    return row_scale * (
        grad_normed - normed * jnp.mean(normed * grad_normed, axis=-1, keepdims=True)
    )


def expert_kernel(extra, experts, base, *refs):
    x_ref, z_ref, gate_w, up_w, down_w = refs[:5]
    back_ref, out_ref, dots_ref, hidden_ref, gate_grad_ref, up_grad_ref, copy_ref = refs[-8:-1]
    gated_ref = refs[-1]
    count, width, size = gate_w.shape
    x = x_ref[:, :width]
    copy_ref[0] = x.T
    ends = x_ref[:, width:].astype(F32)
    lane = lax.broadcasted_iota(jnp.int32, ends.shape, 1)
    dots = jnp.zeros(ends.shape, F32)
    for e in range(count):
        columns = slice(e * size, (e + 1) * size)
        number = base[0] + e
        gate = jnp.sum(
            jnp.where((lane == number) | (lane == number + experts), ends, 0.0),
            axis=1,
            keepdims=True,
        )
        gate_pre = dot(x, gate_w[e])
        up_pre = dot(x, up_w[e])
        down_grad = z_ref[:, columns].astype(F32)
        sigmoid_gate = 1.0 / (1.0 + jnp.exp(-gate_pre))
        activated = gate_pre * sigmoid_gate
        hidden = activated * up_pre
        gated = (hidden * gate).astype(BF16)
        gated_ref[:, columns] = gated
        hidden_ref[0, columns, :] = gated.T
        dots = dots + jnp.where(
            lane == e, jnp.sum(hidden * down_grad, axis=1, keepdims=True), 0.0
        )
        hidden_grad = down_grad * gate
        gate_grad_ref[0, :, columns] = (
            hidden_grad * up_pre * sigmoid_gate * (1.0 + gate_pre * (1.0 - sigmoid_gate))
        ).astype(BF16)
        up_grad_ref[0, :, columns] = (hidden_grad * activated).astype(BF16)
    dots_ref[...] = dots
    tile = min(512, width)
    for start in range(0, width, tile):
        rows = slice(start, start + tile)
        back = jnp.zeros((x.shape[0], tile), F32)
        out = jnp.zeros((x.shape[0], tile), F32)
        for e in range(count):
            columns = slice(e * size, (e + 1) * size)
            back = back + dot_nt(gate_grad_ref[0, :, columns], gate_w[e, rows, :])
            back = back + dot_nt(up_grad_ref[0, :, columns], up_w[e, rows, :])
            out = out + dot(gated_ref[:, columns], down_w[e, :, rows])
        back_ref[:, rows] = back.astype(BF16)
        out_ref[:, rows] = out.astype(BF16)


def expert_products(base, x, z, gate_w, up_w, down_w, slots, slot, kept, experts):
    rows, wide = x.shape
    count, width, size = gate_w.shape
    extra = wide - width
    block = min(256, rows)
    hidden = count * size

    def whole(array):
        return pl.BlockSpec(
            array.shape, lambda i, base: (0, 0, 0), pipeline_mode=pl.Buffered(1)
        )

    def by_rows(columns):
        return pl.BlockSpec((block, columns), lambda i, base: (i, 0))

    def in_slot(columns):
        return pl.BlockSpec((1, block, columns), lambda i, base: (slot, i, 0))

    def turned_in_slot(columns):
        return pl.BlockSpec((1, columns, block), lambda i, base: (slot, 0, i))

    kept_shapes = [
        jax.ShapeDtypeStruct((slots, hidden, rows), BF16),
        jax.ShapeDtypeStruct((slots, rows, hidden), BF16),
        jax.ShapeDtypeStruct((slots, rows, hidden), BF16),
        jax.ShapeDtypeStruct((slots, width, rows), BF16),
    ]
    results = pl.pallas_call(
        functools.partial(expert_kernel, extra, experts),
        out_shape=[
            jax.ShapeDtypeStruct((rows, width), BF16),
            jax.ShapeDtypeStruct((rows, width), BF16),
            jax.ShapeDtypeStruct((rows, extra), F32),
        ]
        + kept_shapes,
        grid_spec=pltpu.PrefetchScalarGridSpec(
            num_scalar_prefetch=1,
            grid=(rows // block,),
            in_specs=[by_rows(wide), by_rows(hidden), whole(gate_w), whole(up_w), whole(down_w)]
            + [pl.BlockSpec(memory_space=pl.ANY)] * len(kept),
            out_specs=[by_rows(width), by_rows(width), by_rows(extra)]
            + [turned_in_slot(hidden), in_slot(hidden), in_slot(hidden), turned_in_slot(width)],
            scratch_shapes=[pltpu.VMEM((block, hidden), BF16)],
        ),
        input_output_aliases={6 + i: 3 + i for i in range(len(kept))},
        cost_estimate=pl.CostEstimate(
            flops=10 * rows * width * hidden,
            bytes_accessed=6 * width * hidden + 2 * rows * (4 * width + 4 * hidden),
            transcendentals=rows * hidden,
        ),
        compiler_params=pltpu.CompilerParams(vmem_limit_bytes=60 * 1024 * 1024),
    )(base, x, z, gate_w, up_w, down_w, *kept)
    return results[0], results[1], results[2], tuple(results[3:])


def wide_kernel(left, right, out_ref):
    count, width, size = out_ref.shape
    tile = min(512, width)
    for start in range(0, width, tile):
        rows = slice(start, start + tile)
        part = dot(left[0, rows, :], right[0])

        @pl.when(pl.program_id(0) == 0)
        def _():
            for e in range(count):
                out_ref[e, rows, :] = part[:, e * size : (e + 1) * size]

        @pl.when(pl.program_id(0) > 0)
        def _():
            for e in range(count):
                out_ref[e, rows, :] += part[:, e * size : (e + 1) * size]


def wide_products(turned, grads, count):
    slots, width, rows = turned.shape
    hidden = grads.shape[2]
    size = hidden // count
    return pl.pallas_call(
        wide_kernel,
        out_shape=jax.ShapeDtypeStruct((count, width, size), F32),
        grid=(slots,),
        in_specs=[
            pl.BlockSpec((1, width, rows), lambda k: (k, 0, 0)),
            pl.BlockSpec((1, rows, hidden), lambda k: (k, 0, 0)),
        ],
        out_specs=pl.BlockSpec((count, width, size), lambda k: (0, 0, 0)),
        cost_estimate=pl.CostEstimate(
            flops=2 * slots * rows * width * hidden,
            bytes_accessed=2 * slots * rows * (width + hidden) + 4 * width * hidden,
            transcendentals=0,
        ),
        compiler_params=pltpu.CompilerParams(vmem_limit_bytes=60 * 1024 * 1024),
    )(turned, grads)


def down_kernel(spans, has_first, left, *refs):
    out_ref = refs[-1]
    step = pl.program_id(0)
    width = out_ref.shape[1]
    tile = min(512, width)
    for index, (begin, end) in enumerate(spans):

        @pl.when((step >= begin) & (step < end))
        def _():
            for start in range(0, width, tile):
                columns = slice(start, start + tile)
                part = dot(left[0], refs[index][0, :, columns])
                if begin > 0:
                    out_ref[:, columns] += part
                elif has_first:
                    out_ref[:, columns] = refs[-2][:, columns] + part
                else:
                    out_ref[:, columns] = part


def down_products(turned, slot, arrays, first=None):
    _, hidden, rows = turned.shape
    width = arrays[0].shape[2]
    spans, count = [], 0
    for array in arrays:
        spans.append((count, count + array.shape[0]))
        count += array.shape[0]

    def member(begin, end):
        return pl.BlockSpec(
            (1, rows, width),
            lambda k: (jnp.clip(k - begin, 0, end - begin - 1), 0, 0),
            pipeline_mode=pl.Buffered(1 if end - begin == 1 else 2),
        )

    constant = pl.BlockSpec((hidden, width), lambda k: (0, 0), pipeline_mode=pl.Buffered(1))
    return pl.pallas_call(
        functools.partial(down_kernel, spans, first is not None),
        out_shape=jax.ShapeDtypeStruct((hidden, width), F32),
        grid=(count,),
        in_specs=[pl.BlockSpec((1, hidden, rows), lambda k: (slot + k, 0, 0))]
        + [member(*span) for span in spans]
        + ([constant] if first is not None else []),
        out_specs=pl.BlockSpec((hidden, width), lambda k: (0, 0)),
        cost_estimate=pl.CostEstimate(
            flops=2 * count * rows * width * hidden,
            bytes_accessed=2 * count * rows * (width + hidden) + 4 * width * hidden,
            transcendentals=0,
        ),
        compiler_params=pltpu.CompilerParams(vmem_limit_bytes=60 * 1024 * 1024),
    )(turned, *arrays, *(() if first is None else (first,)))


def swap_rows(grad):
    count = lax.axis_size("fsdp")
    core = lax.axis_index("fsdp") % 2
    blocks = grad.reshape(count // 2, 2, grad.shape[0] // count, grad.shape[1])
    return (
        lax.dynamic_index_in_dim(blocks, core, 1, keepdims=False),
        swap_core(lax.dynamic_index_in_dim(blocks, 1 - core, 1, keepdims=False)),
    )


def sum_rows(mine, arrived):
    nodes = mine.shape[0]
    node = lax.axis_index("fsdp") // 2

    def part(step):
        place = (node + step) % nodes
        return plus(
            lax.dynamic_index_in_dim(mine, place, 0, keepdims=False),
            lax.dynamic_index_in_dim(arrived, place, 0, keepdims=False),
        )

    total = part(0)
    for step in range(1, nodes):
        total = total + shift_node(part(step).astype(BF16), step).astype(F32)
    return total


def shards(
    tokens,
    cotangent,
    routes,
    gain_attn,
    w_query,
    w_key,
    w_value,
    gain_query,
    gain_key,
    w_out,
    gain_moe,
    w_router,
    w_gate,
    w_up,
    w_down,
):
    tp_count = lax.axis_size("tp")
    tp_rank = lax.axis_index("tp")
    fsdp_count = lax.axis_size("fsdp")
    fsdp_rank = lax.axis_index("fsdp")
    nodes = fsdp_count // 2
    piece, model_width = tokens.shape
    seq_len = piece * tp_count
    local_width = w_query.shape[1]
    head_count = local_width // HEAD_DIM
    expert_count = w_router.shape[1]
    local_experts, _, hidden_slice = w_gate.shape
    hidden_all = local_experts * hidden_slice
    extra = -(-2 * expert_count // 128) * 128
    scale_factor = HEAD_DIM ** (-0.5)
    head_shape = (seq_len, head_count, HEAD_DIM)
    column_start = tp_rank * local_width

    small = gather_small(
        jnp.concatenate(
            [gain_attn[None], gain_moe[None], gain_query[None], gain_key[None], w_router.T], axis=0
        )
    )
    attn_gain, moe_gain = small[0].astype(F32), small[1].astype(F32)
    local_gains = lax.dynamic_slice_in_dim(small[2:4], column_start, local_width, 1).astype(F32)
    local_qgain, local_kgain = local_gains[0], local_gains[1]
    router_w = small[4:]
    dense_w = lax.all_gather(
        jnp.concatenate([w_query, w_key, w_value, w_out.T], axis=1), "fsdp", axis=0, tiled=True
    )
    dense_w = after(dense_w, tokens)
    qkv_w, out_w = dense_w[:, : 3 * local_width], dense_w[:, 3 * local_width :]
    down_w = w_down.reshape(hidden_all, model_width)

    residual_in = tokens.astype(F32)
    normed_one, scale_one = norm_rows(residual_in)
    first_in = (normed_one * attn_gain).astype(BF16)
    first_all = gather_halves(first_in)

    early = after(cotangent, dense_w, first_all)
    grad_own = lax.all_gather(early, "tp", axis=0, tiled=True)
    qkv_raw = dot(first_all, qkv_w)
    around = around_nodes(early, qkv_raw)
    query_raw = qkv_raw[:, :local_width]
    key_raw = qkv_raw[:, local_width : 2 * local_width]
    value_raw = qkv_raw[:, 2 * local_width :]
    squares = sum_tp(
        jnp.stack([jnp.sum(query_raw * query_raw, axis=-1), jnp.sum(key_raw * key_raw, axis=-1)])
    )
    query_scale = lax.rsqrt(squares[0] / model_width + EPSILON)[:, None]
    key_scale = lax.rsqrt(squares[1] / model_width + EPSILON)[:, None]
    positions = jnp.arange(seq_len, dtype=jnp.int32)
    cosine, sine_table = rope_tables(positions, HEAD_DIM)
    query_normed = (query_raw * query_scale * local_qgain).reshape(head_shape)
    key_normed = (key_raw * key_scale * local_kgain).reshape(head_shape)
    query_bf = (query_normed * cosine + rotate(query_normed) * sine_table).astype(BF16)
    key_bf = (key_normed * cosine + rotate(key_normed) * sine_table).astype(BF16)
    value_bf = value_raw.astype(BF16).reshape(head_shape)
    block_rows = min(512, seq_len)
    block_count = seq_len // block_rows

    def block_of(array, block_index):
        return array[block_index * block_rows : (block_index + 1) * block_rows]

    def block_scores(block_index):
        query_block = block_of(query_bf, block_index)
        scores = (
            jnp.einsum("qhd,khd->hqk", query_block, key_bf, preferred_element_type=F32)
            * scale_factor
        )
        causal = block_of(positions, block_index)[:, None] >= positions[None, :]
        return (query_block, jnp.where(causal[None], scores, -1e30), causal)

    attn_blocks, log_totals = [], []
    for block_index in range(block_count):
        query_block, scores, causal = block_scores(block_index)
        top_score = jnp.max(scores, axis=-1, keepdims=True)
        exponent = jnp.exp(scores - top_score)
        row_total = jnp.sum(exponent, axis=-1, keepdims=True)
        attn_probs = (exponent / row_total).astype(BF16)
        attn_blocks.append(
            jnp.einsum("hqk,khd->qhd", attn_probs, value_bf, preferred_element_type=F32)
        )
        log_totals.append(top_score[..., 0] + jnp.log(row_total[..., 0]))
    heads_out = jnp.concatenate(attn_blocks, axis=0).reshape(seq_len, local_width).astype(BF16)
    heads_out = after(heads_out, grad_own, *around[:1], *around[2:])
    attn_sum = scatter_halves(dot_nt(heads_out, out_w).astype(BF16))
    groups = [[0], [1, 3], [2]] if nodes == 4 else [[0]] + [list(range(1, nodes))] * (nodes > 1)
    order = [step for group in groups for step in group]

    def grad_products(own):
        other = swap_core(own)
        flat = [one.reshape(-1, model_width) for one in (own, other)]
        return (own, other) + tuple(
            dot_nt(one, down_w).astype(BF16).reshape(-1, seq_len, hidden_all) for one in flat
        )

    def grad_group(group, *earlier):
        pieces = jnp.stack([around[step - 1] for step in group])
        return grad_products(
            lax.all_gather(after(pieces, *earlier), "tp", axis=1, tiled=True)
        )

    grad_sets = [grad_products(grad_own[None])]
    if nodes > 1:
        grad_sets.append(grad_group(groups[1], attn_blocks[0]))
    attn_sum = after(attn_sum, *grad_sets[0][2:])
    hidden_res = residual_in + attn_sum
    normed_two, scale_two = norm_rows(hidden_res)
    second_in = (normed_two * moe_gain).astype(BF16)

    router_probs = jax.nn.softmax(dot_nt(second_in, router_w), axis=-1)
    own_routes = lax.dynamic_slice_in_dim(routes, tp_rank * piece, piece, 0)
    routed = jnp.any(
        own_routes[:, :, None] == jnp.arange(expert_count, dtype=jnp.int32)[None, None, :], axis=1
    ).astype(F32)
    gates = router_probs * routed
    gates_high = gates.astype(BF16)
    gates_low = (gates - gates_high.astype(F32)).astype(BF16)
    sent = jnp.concatenate(
        [
            second_in,
            gates_high,
            gates_low,
            jnp.zeros((piece, extra - 2 * expert_count), BF16),
        ],
        axis=1,
    )

    sources = around_nodes(sent)
    owns = {0: gather_pieces(sent)}
    for step in order[1:]:
        owns[step] = None if step == 2 else lax.all_gather(
            sources[step - 1], "tp", axis=0, tiled=True
        )
    defer = nodes <= 4
    by_hops = tp_count == 4
    kept, gate_dots, backs, swaps, hops, lasts, returns = (), [], [], [], [], [], []
    outs, outs_back, wholes = [], [], []
    base = jnp.reshape(fsdp_rank * local_experts, (1,)).astype(jnp.int32)

    def one_sequence(place, other, rows):
        nonlocal kept
        index = next(i for i, group in enumerate(groups) if order[place] in group)
        grads = grad_sets[index][3 if other else 2][groups[index].index(order[place])]
        back, out, dots, kept = expert_products(
            base,
            rows,
            grads,
            w_gate,
            w_up,
            w_down,
            2 * nodes,
            place + (nodes if other else 0),
            kept,
            expert_count,
        )
        return back, out, dots[:, :local_experts].T

    def outputs_home(out, *earlier):
        whole = plus(out[0], swap_core(out[1])).astype(BF16)
        wholes.append(whole)
        return [
            lax.psum_scatter(after(whole, *earlier), "tp", scatter_dimension=0, tiled=True)
        ]

    for place, step in enumerate(order):
        own = owns[step]
        other = swap_core(own)
        if by_hops and place > 1:
            own = after(own, *hops[place - 2][2])
            other = after(other, *lasts[place - 2])
        if place == 0:
            own = after(own, *sources[:1], *sources[2:])
            first = one_sequence(place, False, own)
            second = one_sequence(place, True, other)
            mine, others = first, second
            if len(groups) > 2:
                grad_sets.append(grad_group(groups[2], first[0]))
            if 2 in order:
                owns[2] = lax.all_gather(
                    after(sources[1], second[0]), "tp", axis=0, tiled=True
                )
        else:
            if by_hops:
                own = after(own, *hops[place - 1][2])
            first = one_sequence(place, True, other)
            second = one_sequence(place, False, own)
            mine, others = second, first
        if place + 1 < nodes:
            owns[order[place + 1]] = after(owns[order[place + 1]], first[0])
        gate_dots.append((mine[2], others[2]))
        backs.append(mine[0])
        swaps.append(swap_core(others[0]))
        outs.append((mine[1], others[1]))
        if by_hops:
            hops.append(hop_one(mine[0], swaps[-1]))
            lasts.append(hop_two(*hops[-1]))
            returns.append(shift_node(hop_sum(*hops[-1], lasts[-1]).astype(BF16), -step))
        else:
            back_own = plus(mine[0], swaps[-1]).astype(BF16)
            total = lax.psum_scatter(back_own, "tp", scatter_dimension=0, tiled=True)
            returns.append(shift_node(total, -step))
        if not defer:
            outs_back += [shift_node(outputs_home(outs[place])[0], -step)]
            kept = after(kept, outs_back[-1], returns[-1])
    if defer:
        pins = lasts[-1] if by_hops else (returns[-1],)
        for place in range(nodes):
            outs_back += outputs_home(outs[place], *pins)
    hidden_kept, gate_kept, up_kept, rows_kept = kept

    down_w_grad = down_products(hidden_kept, 0, [one[0] for one in grad_sets])
    pins = hops[-1][2] if by_hops else ()
    down_w_grad = down_products(
        after(hidden_kept, *pins), nodes, [one[1] for one in grad_sets], down_w_grad
    )
    if by_hops and nodes > 1:
        returns[-1] = after(returns[-1], down_w_grad)

    back_sum = sum(one.astype(F32) for one in returns)

    def home(place, *earlier):
        if defer:
            outs_back[place] = shift_node(after(outs_back[place], *earlier), -order[place])

    node, core = fsdp_rank // 2, fsdp_rank % 2
    dots = jnp.stack([one[0] for one in gate_dots] + [one[1] for one in gate_dots], axis=1)
    dots = scatter_dots(dots)
    mine, others = dots[:, :nodes], swap_core(dots[:, nodes:])
    pair = jnp.where(core == 0, jnp.stack([mine, others]), jnp.stack([others, mine]))
    placed = jnp.stack(
        [shift_node(pair[:, :, order.index(step)], -step) for step in range(nodes)]
    )
    placed = lax.dynamic_slice_in_dim(
        jnp.concatenate([placed, placed], axis=0), nodes - node, nodes, 0
    )
    prob_grad = placed.reshape(expert_count, piece).T

    grad_out = cotangent.astype(F32)
    prob_grad = prob_grad * routed
    logit_grad = router_probs * (
        prob_grad - jnp.sum(router_probs * prob_grad, axis=-1, keepdims=True)
    )
    router_grad = lax.dot_general(
        logit_grad,
        second_in.astype(F32),
        (((0,), (0,)), ((), ())),
        precision=lax.Precision.HIGHEST,
    )
    second_grad = back_sum + jnp.dot(
        logit_grad, router_w.astype(F32), precision=lax.Precision.HIGHEST
    )
    moe_gain_grad = jnp.sum(normed_two * second_grad, axis=0)
    residual_grad = grad_out + norm_back(normed_two, scale_two, second_grad * moe_gain)

    residual_all = gather_halves(residual_grad.astype(BF16))

    gate_w_grad = wide_products(rows_kept, after(gate_kept, *returns[1:], *wholes), local_experts)
    residual_all = after(residual_all, gate_w_grad)

    out_w_swapped = swap_rows(dot_tn(residual_all, heads_out).astype(BF16))
    out_w_out = sum_rows(*out_w_swapped).T
    early_out = reduce_small(jnp.concatenate([moe_gain_grad[None], router_grad], axis=0))
    heads_grad = dot(residual_all, out_w).astype(BF16).reshape(head_shape)
    key_rot_grad = jnp.zeros(head_shape, F32)
    value_grad = jnp.zeros(head_shape, F32)
    query_blocks_grad = []
    for block_index in range(block_count):
        query_block, scores, causal = block_scores(block_index)
        log_block = log_totals[block_index]
        probs_full = jnp.where(causal[None], jnp.exp(scores - log_block[..., None]), 0.0)
        probs_bf = probs_full.astype(BF16)
        out_block = block_of(heads_grad, block_index)
        if block_index > 0:
            out_block = after(out_block, early_out, out_w_swapped[1])
        value_grad = value_grad + jnp.einsum(
            "hqk,qhd->khd", probs_bf, out_block, preferred_element_type=F32
        )
        prob_block_grad = jnp.einsum(
            "qhd,khd->hqk", out_block, value_bf, preferred_element_type=F32
        )
        centre = jnp.sum(probs_full * prob_block_grad, axis=-1, keepdims=True)
        score_grad = (probs_full * (prob_block_grad - centre)).astype(BF16)
        query_blocks_grad.append(
            jnp.einsum("hqk,khd->qhd", score_grad, key_bf, preferred_element_type=F32)
            * scale_factor
        )
        key_rot_grad = (
            key_rot_grad
            + jnp.einsum("hqk,qhd->khd", score_grad, query_block, preferred_element_type=F32)
            * scale_factor
        )
    query_rot_grad = jnp.concatenate(query_blocks_grad, axis=0)
    query_norm_grad = (query_rot_grad * cosine + rotate_back(query_rot_grad * sine_table)).reshape(
        seq_len, local_width
    )
    key_norm_grad = (key_rot_grad * cosine + rotate_back(key_rot_grad * sine_table)).reshape(
        seq_len, local_width
    )
    qgain_local = jnp.sum(query_raw * query_scale * query_norm_grad, axis=0)
    kgain_local = jnp.sum(key_raw * key_scale * key_norm_grad, axis=0)
    query_inner = query_norm_grad * local_qgain
    key_inner = key_norm_grad * local_kgain
    dots = sum_tp(
        jnp.stack(
            [jnp.sum(query_raw * query_inner, axis=-1), jnp.sum(key_raw * key_inner, axis=-1)]
        )
    )
    query_raw_grad = (
        query_scale * query_inner - query_raw * query_scale**3 * dots[0][:, None] / model_width
    ).astype(BF16)
    key_raw_grad = (
        key_scale * key_inner - key_raw * key_scale**3 * dots[1][:, None] / model_width
    ).astype(BF16)
    value_raw_grad = value_grad.reshape(seq_len, local_width).astype(BF16)
    qkv_grad = jnp.concatenate([query_raw_grad, key_raw_grad, value_raw_grad], axis=1)
    qkv_grad = after(qkv_grad, out_w_out)
    first_part = dot_nt(qkv_grad, qkv_w).astype(BF16)
    first_grad = scatter_halves(first_part)
    for place in range(nodes):
        home(place, query_blocks_grad[0] if place == 1 else first_part)
    output = (hidden_res + sum(one.astype(F32) for one in outs_back)).astype(BF16)
    qkv_w_grad = dot_tn(first_all, qkv_grad).astype(BF16)
    up_w_grad = wide_products(rows_kept, after(up_kept, first_part, qkv_w_grad), local_experts)
    down_w_grad = down_w_grad.reshape(local_experts, hidden_slice, model_width)

    attn_gain_grad = jnp.sum(normed_one * first_grad, axis=0)
    input_grad = residual_grad + norm_back(normed_one, scale_one, first_grad * attn_gain)

    qkv_out = sum_rows(*swap_rows(qkv_w_grad))

    def widen(grad):
        return lax.dynamic_update_slice_in_dim(
            jnp.zeros((1, model_width), F32), grad[None], column_start, 1
        )

    late_out = reduce_small(
        jnp.concatenate(
            [attn_gain_grad[None], widen(qgain_local), widen(kgain_local)], axis=0
        )
    )
    return (
        output,
        input_grad,
        late_out[0],
        qkv_out[:, :local_width],
        qkv_out[:, local_width : 2 * local_width],
        qkv_out[:, 2 * local_width :],
        late_out[1],
        late_out[2],
        out_w_out,
        early_out[0],
        early_out[1:].T,
        gate_w_grad,
        up_w_grad,
        down_w_grad,
    )


def solution(mesh):
    placed = (
        P(("fsdp", "tp"), None),
        P(("fsdp", "tp"), None),
        P("fsdp", None),
        P("fsdp"),
        P("fsdp", "tp"),
        P("fsdp", "tp"),
        P("fsdp", "tp"),
        P("fsdp"),
        P("fsdp"),
        P("tp", "fsdp"),
        P("fsdp"),
        P("fsdp", None),
        P("fsdp", None, "tp"),
        P("fsdp", None, "tp"),
        P("fsdp", "tp", None),
    )
    return jax.shard_map(
        shards,
        mesh=mesh,
        in_specs=placed,
        out_specs=(
            P(("fsdp", "tp"), None),
            P(("fsdp", "tp"), None),
            P("fsdp"),
            P("fsdp", "tp"),
            P("fsdp", "tp"),
            P("fsdp", "tp"),
            P("fsdp"),
            P("fsdp"),
            P("tp", "fsdp"),
            P("fsdp"),
            P("fsdp", None),
            P("fsdp", None, "tp"),
            P("fsdp", None, "tp"),
            P("fsdp", "tp", None),
        ),
        check_vma=False,
    )
```

```python
import functools

import jax
import jax.numpy as jnp
from jax import lax
from jax.experimental import pallas as pl
from jax.experimental.pallas import tpu as pltpu
from jax.sharding import PartitionSpec as P

HEAD_DIM = 128
EPSILON = 1e-05
ROPE_BASE = 10000.0
F32 = jnp.float32
BF16 = jnp.bfloat16


def dot(a, b):
    return jnp.dot(a, b, preferred_element_type=F32)


def dot_nt(a, b):
    return lax.dot_general(a, b, (((1,), (1,)), ((), ())), preferred_element_type=F32)


def dot_tn(a, b):
    return lax.dot_general(a, b, (((0,), (0,)), ((), ())), preferred_element_type=F32)


def swap_core(operand):
    count = lax.axis_size("fsdp")
    return lax.ppermute(operand, "fsdp", [(i, i ^ 1) for i in range(count)])


def shift_node(operand, step):
    count = lax.axis_size("fsdp")
    nodes = count // 2
    if step % nodes == 0:
        return operand
    return lax.ppermute(
        operand, "fsdp", [(i, ((i // 2 + step) % nodes) * 2 + i % 2) for i in range(count)]
    )


def around_nodes(operand, *between):
    count = lax.axis_size("fsdp") // 2
    pieces = []
    for step in range(1, count - 1):
        pieces.append(shift_node(after(pieces[-1], *between) if pieces else operand, 1))
    if count > 1:
        pieces.append(shift_node(operand, -1))
    return pieces


def swap_tp(operand, mask):
    count = lax.axis_size("tp")
    return lax.ppermute(operand, "tp", [(i, i ^ mask) for i in range(count)])


def after(operand, *earlier):
    return lax.optimization_barrier((operand,) + earlier)[0]


def gather_halves(operand):
    if lax.axis_size("tp") != 4:
        return lax.all_gather(operand, "tp", axis=0, tiled=True)
    rows = operand.shape[0]
    half = rows // 2
    a, b = operand[:half], operand[half:]
    a1 = swap_tp(a, 1)
    b2 = swap_tp(b, 2)
    b1 = swap_tp(b, 1)
    a2 = swap_tp(a, 2)
    a3 = swap_tp(a1, 2)
    b3 = swap_tp(b2, 1)
    rank = lax.axis_index("tp")
    placed = jnp.zeros((4 * rows,) + operand.shape[1:], operand.dtype)
    for mask, part, offset in (
        (0, operand, 0),
        (1, a1, 0),
        (1, b1, half),
        (2, a2, 0),
        (2, b2, half),
        (3, a3, 0),
        (3, b3, half),
    ):
        placed = lax.dynamic_update_slice_in_dim(placed, part, (rank ^ mask) * rows + offset, 0)
    return placed


def gather_pieces(operand):
    if lax.axis_size("tp") != 4:
        return lax.all_gather(operand, "tp", axis=0, tiled=True)
    one = swap_tp(operand, 1)
    two = swap_tp(operand, 2)
    three = swap_tp(one, 2)
    rank = lax.axis_index("tp")
    placed = jnp.zeros((4,) + operand.shape, operand.dtype)
    for mask, part in enumerate((operand, one, two, three)):
        placed = lax.dynamic_update_slice_in_dim(placed, part[None], rank ^ mask, 0)
    return placed.reshape(-1, operand.shape[1])


def plus(mine, other):
    return mine.astype(F32) + other.astype(F32)


def hop_one(operand, other=None):
    rows = operand.shape[0] // 4
    half = rows // 2
    rank = lax.axis_index("tp")

    def part(mask, offset):
        start = (rank ^ mask) * rows + offset
        mine = lax.dynamic_slice_in_dim(operand, start, half, 0)
        if other is None:
            return mine
        return plus(mine, lax.dynamic_slice_in_dim(other, start, half, 0))

    arrived = (
        swap_tp(part(3, 0).astype(BF16), 2),
        swap_tp(part(3, half).astype(BF16), 1),
        swap_tp(part(2, 0).astype(BF16), 2),
        swap_tp(part(1, half).astype(BF16), 1),
    )
    return part, half, arrived


def hop_two(part, half, arrived):
    a3, b3, _, _ = arrived
    return (
        swap_tp(plus(part(1, 0), a3).astype(BF16), 1),
        swap_tp(plus(part(2, half), b3).astype(BF16), 2),
    )


def hop_sum(part, half, arrived, last):
    _, _, a2, b1 = arrived
    ra = plus(plus(part(0, 0), a2), last[0])
    rb = plus(plus(part(0, half), b1), last[1])
    return jnp.concatenate([ra, rb], axis=0)


def scatter_halves(operand):
    if lax.axis_size("tp") != 4:
        return lax.psum_scatter(operand, "tp", scatter_dimension=0, tiled=True).astype(F32)
    first = hop_one(operand)
    return hop_sum(*first, hop_two(*first))


def scatter_dots(operand):
    if lax.axis_size("tp") != 4:
        return lax.psum_scatter(operand, "tp", scatter_dimension=2, tiled=True)
    rank = lax.axis_index("tp")
    size = operand.shape[2] // 4
    total = lax.dynamic_slice_in_dim(operand, rank * size, size, 2)
    for mask in (1, 2, 3):
        total = total + swap_tp(
            lax.dynamic_slice_in_dim(operand, (rank ^ mask) * size, size, 2), mask
        )
    return total


def gather_small(operand):
    count = lax.axis_size("fsdp")
    nodes = count // 2
    rank = lax.axis_index("fsdp")
    node, core = rank // 2, rank % 2
    other = swap_core(operand)
    pair = jnp.where(core == 0, jnp.stack([operand, other]), jnp.stack([other, operand]))
    around = [shift_node(pair, step) for step in range(nodes - 1, 0, -1)] + [pair]
    both = jnp.concatenate(around + around, axis=0)
    placed = lax.dynamic_slice_in_dim(both, 2 * (nodes - 1 - node), count, 0)
    return placed.transpose(1, 0, 2).reshape(operand.shape[0], -1)


def reduce_small(operand):
    count = lax.axis_size("fsdp")
    nodes = count // 2
    rank = lax.axis_index("fsdp")
    node, core = rank // 2, rank % 2
    blocks = operand.reshape(operand.shape[0], nodes, 2, -1).transpose(2, 1, 0, 3)
    mine = lax.dynamic_index_in_dim(blocks, core, 0, keepdims=False)
    mine = mine + swap_core(lax.dynamic_index_in_dim(blocks, 1 - core, 0, keepdims=False))
    total = lax.dynamic_index_in_dim(mine, node, 0, keepdims=False)
    for step in range(1, nodes):
        part = lax.dynamic_index_in_dim(mine, (node + step) % nodes, 0, keepdims=False)
        total = total + shift_node(part, step)
    return sum_tp(total)


def sum_tp(operand):
    if lax.axis_size("tp") != 4:
        return lax.psum(operand, "tp")
    return (operand + swap_tp(operand, 1)) + (swap_tp(operand, 2) + swap_tp(operand, 3))


def rope_tables(positions, columns):
    halfway = columns // 2
    frequency = ROPE_BASE ** (-2.0 * jnp.arange(halfway).astype(F32) / columns)
    angles = positions.astype(F32)[:, None] * frequency[None, :]
    angles = jnp.concatenate([angles, angles], axis=-1)
    return (jnp.cos(angles)[:, None, :], jnp.sin(angles)[:, None, :])


def rotate(tensor):
    halfway = tensor.shape[-1] // 2
    return jnp.concatenate([-tensor[..., halfway:], tensor[..., :halfway]], axis=-1)


def rotate_back(tensor):
    halfway = tensor.shape[-1] // 2
    return jnp.concatenate([tensor[..., halfway:], -tensor[..., :halfway]], axis=-1)


def norm_rows(tensor):
    row_scale = lax.rsqrt(jnp.mean(tensor * tensor, axis=-1, keepdims=True) + EPSILON)
    return (tensor * row_scale, row_scale)


def norm_back(normed, row_scale, grad_normed):
    return row_scale * (
        grad_normed - normed * jnp.mean(normed * grad_normed, axis=-1, keepdims=True)
    )


def expert_kernel(extra, experts, base, *refs):
    x_ref, z_ref, gate_w, up_w, down_w = refs[:5]
    back_ref, out_ref, dots_ref, hidden_ref, gate_grad_ref, up_grad_ref, copy_ref = refs[-8:-1]
    gated_ref = refs[-1]
    count, width, size = gate_w.shape
    x = x_ref[:, :width]
    copy_ref[0] = x.T
    ends = x_ref[:, width:].astype(F32)
    lane = lax.broadcasted_iota(jnp.int32, ends.shape, 1)
    dots = jnp.zeros(ends.shape, F32)
    for e in range(count):
        columns = slice(e * size, (e + 1) * size)
        number = base[0] + e
        gate = jnp.sum(
            jnp.where((lane == number) | (lane == number + experts), ends, 0.0),
            axis=1,
            keepdims=True,
        )
        gate_pre = dot(x, gate_w[e])
        up_pre = dot(x, up_w[e])
        down_grad = z_ref[:, columns].astype(F32)
        sigmoid_gate = 1.0 / (1.0 + jnp.exp(-gate_pre))
        activated = gate_pre * sigmoid_gate
        hidden = activated * up_pre
        gated = (hidden * gate).astype(BF16)
        gated_ref[:, columns] = gated
        hidden_ref[0, columns, :] = gated.T
        dots = dots + jnp.where(
            lane == e, jnp.sum(hidden * down_grad, axis=1, keepdims=True), 0.0
        )
        hidden_grad = down_grad * gate
        gate_grad_ref[0, :, columns] = (
            hidden_grad * up_pre * sigmoid_gate * (1.0 + gate_pre * (1.0 - sigmoid_gate))
        ).astype(BF16)
        up_grad_ref[0, :, columns] = (hidden_grad * activated).astype(BF16)
    dots_ref[...] = dots
    tile = min(512, width)
    for start in range(0, width, tile):
        rows = slice(start, start + tile)
        back = jnp.zeros((x.shape[0], tile), F32)
        out = jnp.zeros((x.shape[0], tile), F32)
        for e in range(count):
            columns = slice(e * size, (e + 1) * size)
            back = back + dot_nt(gate_grad_ref[0, :, columns], gate_w[e, rows, :])
            back = back + dot_nt(up_grad_ref[0, :, columns], up_w[e, rows, :])
            out = out + dot(gated_ref[:, columns], down_w[e, :, rows])
        back_ref[:, rows] = back.astype(BF16)
        out_ref[:, rows] = out.astype(BF16)


def expert_products(base, x, z, gate_w, up_w, down_w, slots, slot, kept, experts):
    rows, wide = x.shape
    count, width, size = gate_w.shape
    extra = wide - width
    block = min(256, rows)
    hidden = count * size

    def whole(array):
        return pl.BlockSpec(
            array.shape, lambda i, base: (0, 0, 0), pipeline_mode=pl.Buffered(1)
        )

    def by_rows(columns):
        return pl.BlockSpec((block, columns), lambda i, base: (i, 0))

    def in_slot(columns):
        return pl.BlockSpec((1, block, columns), lambda i, base: (slot, i, 0))

    def turned_in_slot(columns):
        return pl.BlockSpec((1, columns, block), lambda i, base: (slot, 0, i))

    kept_shapes = [
        jax.ShapeDtypeStruct((slots, hidden, rows), BF16),
        jax.ShapeDtypeStruct((slots, rows, hidden), BF16),
        jax.ShapeDtypeStruct((slots, rows, hidden), BF16),
        jax.ShapeDtypeStruct((slots, width, rows), BF16),
    ]
    results = pl.pallas_call(
        functools.partial(expert_kernel, extra, experts),
        out_shape=[
            jax.ShapeDtypeStruct((rows, width), BF16),
            jax.ShapeDtypeStruct((rows, width), BF16),
            jax.ShapeDtypeStruct((rows, extra), F32),
        ]
        + kept_shapes,
        grid_spec=pltpu.PrefetchScalarGridSpec(
            num_scalar_prefetch=1,
            grid=(rows // block,),
            in_specs=[by_rows(wide), by_rows(hidden), whole(gate_w), whole(up_w), whole(down_w)]
            + [pl.BlockSpec(memory_space=pl.ANY)] * len(kept),
            out_specs=[by_rows(width), by_rows(width), by_rows(extra)]
            + [turned_in_slot(hidden), in_slot(hidden), in_slot(hidden), turned_in_slot(width)],
            scratch_shapes=[pltpu.VMEM((block, hidden), BF16)],
        ),
        input_output_aliases={6 + i: 3 + i for i in range(len(kept))},
        cost_estimate=pl.CostEstimate(
            flops=10 * rows * width * hidden,
            bytes_accessed=6 * width * hidden + 2 * rows * (4 * width + 4 * hidden),
            transcendentals=rows * hidden,
        ),
        compiler_params=pltpu.CompilerParams(vmem_limit_bytes=60 * 1024 * 1024),
    )(base, x, z, gate_w, up_w, down_w, *kept)
    return results[0], results[1], results[2], tuple(results[3:])


def wide_kernel(left, right, out_ref):
    count, width, size = out_ref.shape
    tile = min(512, width)
    for start in range(0, width, tile):
        rows = slice(start, start + tile)
        part = dot(left[0, rows, :], right[0])

        @pl.when(pl.program_id(0) == 0)
        def _():
            for e in range(count):
                out_ref[e, rows, :] = part[:, e * size : (e + 1) * size]

        @pl.when(pl.program_id(0) > 0)
        def _():
            for e in range(count):
                out_ref[e, rows, :] += part[:, e * size : (e + 1) * size]


def wide_products(turned, grads, count):
    slots, width, rows = turned.shape
    hidden = grads.shape[2]
    size = hidden // count
    return pl.pallas_call(
        wide_kernel,
        out_shape=jax.ShapeDtypeStruct((count, width, size), F32),
        grid=(slots,),
        in_specs=[
            pl.BlockSpec((1, width, rows), lambda k: (k, 0, 0)),
            pl.BlockSpec((1, rows, hidden), lambda k: (k, 0, 0)),
        ],
        out_specs=pl.BlockSpec((count, width, size), lambda k: (0, 0, 0)),
        cost_estimate=pl.CostEstimate(
            flops=2 * slots * rows * width * hidden,
            bytes_accessed=2 * slots * rows * (width + hidden) + 4 * width * hidden,
            transcendentals=0,
        ),
        compiler_params=pltpu.CompilerParams(vmem_limit_bytes=60 * 1024 * 1024),
    )(turned, grads)


def down_kernel(spans, has_first, left, *refs):
    out_ref = refs[-1]
    step = pl.program_id(0)
    width = out_ref.shape[1]
    tile = min(512, width)
    for index, (begin, end) in enumerate(spans):

        @pl.when((step >= begin) & (step < end))
        def _():
            for start in range(0, width, tile):
                columns = slice(start, start + tile)
                part = dot(left[0], refs[index][0, :, columns])
                if begin > 0:
                    out_ref[:, columns] += part
                elif has_first:
                    out_ref[:, columns] = refs[-2][:, columns] + part
                else:
                    out_ref[:, columns] = part


def down_products(turned, slot, arrays, first=None):
    _, hidden, rows = turned.shape
    width = arrays[0].shape[2]
    spans, count = [], 0
    for array in arrays:
        spans.append((count, count + array.shape[0]))
        count += array.shape[0]

    def member(begin, end):
        return pl.BlockSpec(
            (1, rows, width),
            lambda k: (jnp.clip(k - begin, 0, end - begin - 1), 0, 0),
            pipeline_mode=pl.Buffered(1 if end - begin == 1 else 2),
        )

    constant = pl.BlockSpec((hidden, width), lambda k: (0, 0), pipeline_mode=pl.Buffered(1))
    return pl.pallas_call(
        functools.partial(down_kernel, spans, first is not None),
        out_shape=jax.ShapeDtypeStruct((hidden, width), F32),
        grid=(count,),
        in_specs=[pl.BlockSpec((1, hidden, rows), lambda k: (slot + k, 0, 0))]
        + [member(*span) for span in spans]
        + ([constant] if first is not None else []),
        out_specs=pl.BlockSpec((hidden, width), lambda k: (0, 0)),
        cost_estimate=pl.CostEstimate(
            flops=2 * count * rows * width * hidden,
            bytes_accessed=2 * count * rows * (width + hidden) + 4 * width * hidden,
            transcendentals=0,
        ),
        compiler_params=pltpu.CompilerParams(vmem_limit_bytes=60 * 1024 * 1024),
    )(turned, *arrays, *(() if first is None else (first,)))


def swap_rows(grad):
    count = lax.axis_size("fsdp")
    core = lax.axis_index("fsdp") % 2
    blocks = grad.reshape(count // 2, 2, grad.shape[0] // count, grad.shape[1])
    return (
        lax.dynamic_index_in_dim(blocks, core, 1, keepdims=False),
        swap_core(lax.dynamic_index_in_dim(blocks, 1 - core, 1, keepdims=False)),
    )


def sum_rows(mine, arrived):
    nodes = mine.shape[0]
    node = lax.axis_index("fsdp") // 2

    def part(step):
        place = (node + step) % nodes
        return plus(
            lax.dynamic_index_in_dim(mine, place, 0, keepdims=False),
            lax.dynamic_index_in_dim(arrived, place, 0, keepdims=False),
        )

    total = part(0)
    for step in range(1, nodes):
        total = total + shift_node(part(step).astype(BF16), step).astype(F32)
    return total


def shards(
    tokens,
    cotangent,
    routes,
    gain_attn,
    w_query,
    w_key,
    w_value,
    gain_query,
    gain_key,
    w_out,
    gain_moe,
    w_router,
    w_gate,
    w_up,
    w_down,
):
    tp_count = lax.axis_size("tp")
    tp_rank = lax.axis_index("tp")
    fsdp_count = lax.axis_size("fsdp")
    fsdp_rank = lax.axis_index("fsdp")
    nodes = fsdp_count // 2
    piece, model_width = tokens.shape
    seq_len = piece * tp_count
    local_width = w_query.shape[1]
    head_count = local_width // HEAD_DIM
    expert_count = w_router.shape[1]
    local_experts, _, hidden_slice = w_gate.shape
    hidden_all = local_experts * hidden_slice
    extra = -(-2 * expert_count // 128) * 128
    scale_factor = HEAD_DIM ** (-0.5)
    head_shape = (seq_len, head_count, HEAD_DIM)
    column_start = tp_rank * local_width

    small = gather_small(
        jnp.concatenate(
            [gain_attn[None], gain_moe[None], gain_query[None], gain_key[None], w_router.T], axis=0
        )
    )
    attn_gain, moe_gain = small[0].astype(F32), small[1].astype(F32)
    local_gains = lax.dynamic_slice_in_dim(small[2:4], column_start, local_width, 1).astype(F32)
    local_qgain, local_kgain = local_gains[0], local_gains[1]
    router_w = small[4:]
    dense_w = lax.all_gather(
        jnp.concatenate([w_query, w_key, w_value, w_out.T], axis=1), "fsdp", axis=0, tiled=True
    )
    dense_w = after(dense_w, tokens)
    qkv_w, out_w = dense_w[:, : 3 * local_width], dense_w[:, 3 * local_width :]
    down_w = w_down.reshape(hidden_all, model_width)

    residual_in = tokens.astype(F32)
    normed_one, scale_one = norm_rows(residual_in)
    first_in = (normed_one * attn_gain).astype(BF16)
    first_all = gather_halves(first_in)

    early = after(cotangent, dense_w, first_all)
    grad_own = lax.all_gather(early, "tp", axis=0, tiled=True)
    qkv_raw = dot(first_all, qkv_w)
    around = around_nodes(early, qkv_raw)
    query_raw = qkv_raw[:, :local_width]
    key_raw = qkv_raw[:, local_width : 2 * local_width]
    value_raw = qkv_raw[:, 2 * local_width :]
    squares = sum_tp(
        jnp.stack([jnp.sum(query_raw * query_raw, axis=-1), jnp.sum(key_raw * key_raw, axis=-1)])
    )
    query_scale = lax.rsqrt(squares[0] / model_width + EPSILON)[:, None]
    key_scale = lax.rsqrt(squares[1] / model_width + EPSILON)[:, None]
    positions = jnp.arange(seq_len, dtype=jnp.int32)
    cosine, sine_table = rope_tables(positions, HEAD_DIM)
    query_normed = (query_raw * query_scale * local_qgain).reshape(head_shape)
    key_normed = (key_raw * key_scale * local_kgain).reshape(head_shape)
    query_bf = (query_normed * cosine + rotate(query_normed) * sine_table).astype(BF16)
    key_bf = (key_normed * cosine + rotate(key_normed) * sine_table).astype(BF16)
    value_bf = value_raw.astype(BF16).reshape(head_shape)
    block_rows = min(512, seq_len)
    block_count = seq_len // block_rows

    def block_of(array, block_index):
        return array[block_index * block_rows : (block_index + 1) * block_rows]

    def block_scores(block_index):
        query_block = block_of(query_bf, block_index)
        scores = (
            jnp.einsum("qhd,khd->hqk", query_block, key_bf, preferred_element_type=F32)
            * scale_factor
        )
        causal = block_of(positions, block_index)[:, None] >= positions[None, :]
        return (query_block, jnp.where(causal[None], scores, -1e30), causal)

    attn_blocks, log_totals = [], []
    for block_index in range(block_count):
        query_block, scores, causal = block_scores(block_index)
        top_score = jnp.max(scores, axis=-1, keepdims=True)
        exponent = jnp.exp(scores - top_score)
        row_total = jnp.sum(exponent, axis=-1, keepdims=True)
        attn_probs = (exponent / row_total).astype(BF16)
        attn_blocks.append(
            jnp.einsum("hqk,khd->qhd", attn_probs, value_bf, preferred_element_type=F32)
        )
        log_totals.append(top_score[..., 0] + jnp.log(row_total[..., 0]))
    heads_out = jnp.concatenate(attn_blocks, axis=0).reshape(seq_len, local_width).astype(BF16)
    heads_out = after(heads_out, grad_own, *around[:1], *around[2:])
    attn_sum = scatter_halves(dot_nt(heads_out, out_w).astype(BF16))
    groups = [[0], [1, 3], [2]] if nodes == 4 else [[0]] + [list(range(1, nodes))] * (nodes > 1)
    order = [step for group in groups for step in group]

    def grad_products(own):
        other = swap_core(own)
        flat = [one.reshape(-1, model_width) for one in (own, other)]
        return (own, other) + tuple(
            dot_nt(one, down_w).astype(BF16).reshape(-1, seq_len, hidden_all) for one in flat
        )

    def grad_group(group, *earlier):
        pieces = jnp.stack([around[step - 1] for step in group])
        return grad_products(
            lax.all_gather(after(pieces, *earlier), "tp", axis=1, tiled=True)
        )

    grad_sets = [grad_products(grad_own[None])]
    if nodes > 1:
        grad_sets.append(grad_group(groups[1], attn_blocks[0]))
    hidden_res = residual_in + attn_sum
    normed_two, scale_two = norm_rows(hidden_res)
    second_in = (normed_two * moe_gain).astype(BF16)

    router_probs = jax.nn.softmax(dot_nt(second_in, router_w), axis=-1)
    own_routes = lax.dynamic_slice_in_dim(routes, tp_rank * piece, piece, 0)
    routed = jnp.any(
        own_routes[:, :, None] == jnp.arange(expert_count, dtype=jnp.int32)[None, None, :], axis=1
    ).astype(F32)
    gates = router_probs * routed
    gates_high = gates.astype(BF16)
    gates_low = (gates - gates_high.astype(F32)).astype(BF16)
    sent = jnp.concatenate(
        [
            second_in,
            gates_high,
            gates_low,
            jnp.zeros((piece, extra - 2 * expert_count), BF16),
        ],
        axis=1,
    )

    sent = after(sent, *grad_sets[0][2:])
    owns = {0: gather_halves(sent)}
    sources = around_nodes(after(sent, owns[0]))
    for step in order[1:]:
        owns[step] = None if step == 2 else lax.all_gather(
            sources[step - 1], "tp", axis=0, tiled=True
        )
    defer = nodes <= 4
    by_hops = tp_count == 4
    kept, gate_dots, backs, swaps, hops, lasts, returns = (), [], [], [], [], [], []
    outs, outs_back, wholes = [], [], []
    base = jnp.reshape(fsdp_rank * local_experts, (1,)).astype(jnp.int32)

    def one_sequence(place, other, rows):
        nonlocal kept
        index = next(i for i, group in enumerate(groups) if order[place] in group)
        grads = grad_sets[index][3 if other else 2][groups[index].index(order[place])]
        back, out, dots, kept = expert_products(
            base,
            rows,
            grads,
            w_gate,
            w_up,
            w_down,
            2 * nodes,
            place + (nodes if other else 0),
            kept,
            expert_count,
        )
        return back, out, dots[:, :local_experts].T

    def outputs_home(out, *earlier):
        whole = plus(out[0], swap_core(out[1])).astype(BF16)
        wholes.append(whole)
        return [
            lax.psum_scatter(after(whole, *earlier), "tp", scatter_dimension=0, tiled=True)
        ]

    for place, step in enumerate(order):
        own = owns[step]
        other = swap_core(own)
        if by_hops and place > 1:
            own = after(own, *hops[place - 2][2])
            other = after(other, *lasts[place - 2])
        if place == 0:
            first = one_sequence(place, False, own)
            second = one_sequence(place, True, other)
            mine, others = first, second
            if len(groups) > 2:
                grad_sets.append(grad_group(groups[2], first[0]))
            if 2 in order:
                owns[2] = lax.all_gather(
                    after(sources[1], second[0]), "tp", axis=0, tiled=True
                )
        else:
            if by_hops:
                own = after(own, *hops[place - 1][2])
            first = one_sequence(place, True, other)
            second = one_sequence(place, False, own)
            mine, others = second, first
        if place + 1 < nodes:
            owns[order[place + 1]] = after(owns[order[place + 1]], first[0])
        gate_dots.append((mine[2], others[2]))
        backs.append(mine[0])
        swaps.append(swap_core(others[0]))
        outs.append((mine[1], others[1]))
        if by_hops and defer and place == nodes - 1:
            hops.append(hop_one(mine[0], swaps[-1]))
        elif by_hops:
            hops.append(hop_one(mine[0], swaps[-1]))
            lasts.append(hop_two(*hops[-1]))
            returns.append(shift_node(hop_sum(*hops[-1], lasts[-1]).astype(BF16), -step))
        else:
            back_own = plus(mine[0], swaps[-1]).astype(BF16)
            total = lax.psum_scatter(back_own, "tp", scatter_dimension=0, tiled=True)
            returns.append(shift_node(total, -step))
        if not defer:
            outs_back += [shift_node(outputs_home(outs[place])[0], -step)]
            kept = after(kept, outs_back[-1], returns[-1])
    hidden_kept, gate_kept, up_kept, rows_kept = kept

    down_w_grad = down_products(hidden_kept, 0, [one[0] for one in grad_sets])
    pins = ()
    if by_hops and defer:
        part, half, arrived = hops[-1]
        arrived = tuple(after(one, down_w_grad) for one in arrived)
        last = hop_two(part, half, arrived)
        pins = arrived
    down_w_grad = down_products(
        after(hidden_kept, *pins), nodes, [one[1] for one in grad_sets], down_w_grad
    )
    if by_hops and defer:
        last = tuple(after(one, down_w_grad) for one in last)
        returns.append(shift_node(hop_sum(part, half, arrived, last).astype(BF16), -order[-1]))
    if defer:
        pins = last if by_hops else (returns[-1],)
        wholes = [plus(after(own, *pins), swap_core(other)).astype(BF16) for own, other in outs]
        pair = lax.psum_scatter(
            jnp.stack(wholes[:2]), "tp", scatter_dimension=1, tiled=True
        )
        outs_back = list(pair) + [
            lax.psum_scatter(whole, "tp", scatter_dimension=0, tiled=True)
            for whole in wholes[2:]
        ]
    back_sum = sum(one.astype(F32) for one in returns)

    def home(place, *earlier):
        if defer:
            outs_back[place] = shift_node(after(outs_back[place], *earlier), -order[place])

    node, core = fsdp_rank // 2, fsdp_rank % 2
    dots = jnp.stack([one[0] for one in gate_dots] + [one[1] for one in gate_dots], axis=1)
    dots = scatter_dots(dots)
    mine, others = dots[:, :nodes], swap_core(dots[:, nodes:])
    pair = jnp.where(core == 0, jnp.stack([mine, others]), jnp.stack([others, mine]))
    placed = jnp.stack(
        [shift_node(pair[:, :, order.index(step)], -step) for step in range(nodes)]
    )
    placed = lax.dynamic_slice_in_dim(
        jnp.concatenate([placed, placed], axis=0), nodes - node, nodes, 0
    )
    prob_grad = placed.reshape(expert_count, piece).T

    grad_out = cotangent.astype(F32)
    prob_grad = prob_grad * routed
    logit_grad = router_probs * (
        prob_grad - jnp.sum(router_probs * prob_grad, axis=-1, keepdims=True)
    )
    router_grad = lax.dot_general(
        logit_grad,
        second_in.astype(F32),
        (((0,), (0,)), ((), ())),
        precision=lax.Precision.HIGHEST,
    )
    second_grad = back_sum + jnp.dot(
        logit_grad, router_w.astype(F32), precision=lax.Precision.HIGHEST
    )
    moe_gain_grad = jnp.sum(normed_two * second_grad, axis=0)
    residual_grad = grad_out + norm_back(normed_two, scale_two, second_grad * moe_gain)

    residual_all = gather_halves(residual_grad.astype(BF16))

    gate_w_grad = wide_products(rows_kept, after(gate_kept, *returns[1:], *wholes), local_experts)
    residual_all = after(residual_all, gate_w_grad)

    out_w_swapped = swap_rows(dot_tn(residual_all, heads_out).astype(BF16))
    out_w_out = sum_rows(*out_w_swapped).T
    early_out = reduce_small(jnp.concatenate([moe_gain_grad[None], router_grad], axis=0))
    heads_grad = dot(residual_all, out_w).astype(BF16).reshape(head_shape)
    key_rot_grad = jnp.zeros(head_shape, F32)
    value_grad = jnp.zeros(head_shape, F32)
    query_blocks_grad = []
    for block_index in range(block_count):
        query_block, scores, causal = block_scores(block_index)
        log_block = log_totals[block_index]
        probs_full = jnp.where(causal[None], jnp.exp(scores - log_block[..., None]), 0.0)
        probs_bf = probs_full.astype(BF16)
        out_block = block_of(heads_grad, block_index)
        if block_index > 0:
            out_block = after(out_block, early_out, out_w_swapped[1])
        value_grad = value_grad + jnp.einsum(
            "hqk,qhd->khd", probs_bf, out_block, preferred_element_type=F32
        )
        prob_block_grad = jnp.einsum(
            "qhd,khd->hqk", out_block, value_bf, preferred_element_type=F32
        )
        centre = jnp.sum(probs_full * prob_block_grad, axis=-1, keepdims=True)
        score_grad = (probs_full * (prob_block_grad - centre)).astype(BF16)
        query_blocks_grad.append(
            jnp.einsum("hqk,khd->qhd", score_grad, key_bf, preferred_element_type=F32)
            * scale_factor
        )
        key_rot_grad = (
            key_rot_grad
            + jnp.einsum("hqk,qhd->khd", score_grad, query_block, preferred_element_type=F32)
            * scale_factor
        )
    query_rot_grad = jnp.concatenate(query_blocks_grad, axis=0)
    query_norm_grad = (query_rot_grad * cosine + rotate_back(query_rot_grad * sine_table)).reshape(
        seq_len, local_width
    )
    key_norm_grad = (key_rot_grad * cosine + rotate_back(key_rot_grad * sine_table)).reshape(
        seq_len, local_width
    )
    qgain_local = jnp.sum(query_raw * query_scale * query_norm_grad, axis=0)
    kgain_local = jnp.sum(key_raw * key_scale * key_norm_grad, axis=0)
    query_inner = query_norm_grad * local_qgain
    key_inner = key_norm_grad * local_kgain
    dots = sum_tp(
        jnp.stack(
            [jnp.sum(query_raw * query_inner, axis=-1), jnp.sum(key_raw * key_inner, axis=-1)]
        )
    )
    query_raw_grad = (
        query_scale * query_inner - query_raw * query_scale**3 * dots[0][:, None] / model_width
    ).astype(BF16)
    key_raw_grad = (
        key_scale * key_inner - key_raw * key_scale**3 * dots[1][:, None] / model_width
    ).astype(BF16)
    value_raw_grad = value_grad.reshape(seq_len, local_width).astype(BF16)
    qkv_grad = jnp.concatenate([query_raw_grad, key_raw_grad, value_raw_grad], axis=1)
    qkv_grad = after(qkv_grad, out_w_out)
    first_part = dot_nt(qkv_grad, qkv_w).astype(BF16)
    first_grad = scatter_halves(first_part)
    for place in range(nodes):
        home(place, (heads_grad, heads_grad, query_blocks_grad[-1], first_grad)[min(place, 3)])
    output = (hidden_res + sum(one.astype(F32) for one in outs_back)).astype(BF16)
    qkv_w_grad = dot_tn(first_all, qkv_grad).astype(BF16)
    up_w_grad = wide_products(rows_kept, after(up_kept, first_part, qkv_w_grad, outs_back[0]), local_experts)
    down_w_grad = down_w_grad.reshape(local_experts, hidden_slice, model_width)

    attn_gain_grad = jnp.sum(normed_one * first_grad, axis=0)
    input_grad = residual_grad + norm_back(normed_one, scale_one, first_grad * attn_gain)

    qkv_out = sum_rows(*swap_rows(qkv_w_grad))

    def widen(grad):
        return lax.dynamic_update_slice_in_dim(
            jnp.zeros((1, model_width), F32), grad[None], column_start, 1
        )

    late_out = reduce_small(
        jnp.concatenate(
            [attn_gain_grad[None], widen(qgain_local), widen(kgain_local)], axis=0
        )
    )
    return (
        output,
        input_grad,
        late_out[0],
        qkv_out[:, :local_width],
        qkv_out[:, local_width : 2 * local_width],
        qkv_out[:, 2 * local_width :],
        late_out[1],
        late_out[2],
        out_w_out,
        early_out[0],
        early_out[1:].T,
        gate_w_grad,
        up_w_grad,
        down_w_grad,
    )


def solution(mesh):
    placed = (
        P(("fsdp", "tp"), None),
        P(("fsdp", "tp"), None),
        P("fsdp", None),
        P("fsdp"),
        P("fsdp", "tp"),
        P("fsdp", "tp"),
        P("fsdp", "tp"),
        P("fsdp"),
        P("fsdp"),
        P("tp", "fsdp"),
        P("fsdp"),
        P("fsdp", None),
        P("fsdp", None, "tp"),
        P("fsdp", None, "tp"),
        P("fsdp", "tp", None),
    )
    return jax.shard_map(
        shards,
        mesh=mesh,
        in_specs=placed,
        out_specs=(
            P(("fsdp", "tp"), None),
            P(("fsdp", "tp"), None),
            P("fsdp"),
            P("fsdp", "tp"),
            P("fsdp", "tp"),
            P("fsdp", "tp"),
            P("fsdp"),
            P("fsdp"),
            P("tp", "fsdp"),
            P("fsdp"),
            P("fsdp", None),
            P("fsdp", None, "tp"),
            P("fsdp", None, "tp"),
            P("fsdp", "tp", None),
        ),
        check_vma=False,
    )
```

```python
import functools

import jax
import jax.numpy as jnp
from jax import lax
from jax.experimental import pallas as pl
from jax.experimental.pallas import tpu as pltpu
from jax.sharding import PartitionSpec as P

HEAD_DIM = 128
EPSILON = 1e-05
ROPE_BASE = 10000.0
F32 = jnp.float32
BF16 = jnp.bfloat16


def dot(a, b):
    return jnp.dot(a, b, preferred_element_type=F32)


def dot_nt(a, b):
    return lax.dot_general(a, b, (((1,), (1,)), ((), ())), preferred_element_type=F32)


def dot_tn(a, b):
    return lax.dot_general(a, b, (((0,), (0,)), ((), ())), preferred_element_type=F32)


def swap_core(operand):
    count = lax.axis_size("fsdp")
    return lax.ppermute(operand, "fsdp", [(i, i ^ 1) for i in range(count)])


def shift_node(operand, step):
    count = lax.axis_size("fsdp")
    nodes = count // 2
    if step % nodes == 0:
        return operand
    return lax.ppermute(
        operand, "fsdp", [(i, ((i // 2 + step) % nodes) * 2 + i % 2) for i in range(count)]
    )


def around_nodes(operand, *between):
    count = lax.axis_size("fsdp") // 2
    pieces = []
    for step in range(1, count - 1):
        pieces.append(shift_node(after(pieces[-1], *between) if pieces else operand, 1))
    if count > 1:
        pieces.append(shift_node(operand, -1))
    return pieces


def swap_tp(operand, mask):
    count = lax.axis_size("tp")
    return lax.ppermute(operand, "tp", [(i, i ^ mask) for i in range(count)])


def after(operand, *earlier):
    return lax.optimization_barrier((operand,) + earlier)[0]


def gather_halves(operand):
    if lax.axis_size("tp") != 4:
        return lax.all_gather(operand, "tp", axis=0, tiled=True)
    rows = operand.shape[0]
    half = rows // 2
    a, b = operand[:half], operand[half:]
    a1 = swap_tp(a, 1)
    b2 = swap_tp(b, 2)
    b1 = swap_tp(b, 1)
    a2 = swap_tp(a, 2)
    a3 = swap_tp(a1, 2)
    b3 = swap_tp(b2, 1)
    rank = lax.axis_index("tp")
    placed = jnp.zeros((4 * rows,) + operand.shape[1:], operand.dtype)
    for mask, part, offset in (
        (0, operand, 0),
        (1, a1, 0),
        (1, b1, half),
        (2, a2, 0),
        (2, b2, half),
        (3, a3, 0),
        (3, b3, half),
    ):
        placed = lax.dynamic_update_slice_in_dim(placed, part, (rank ^ mask) * rows + offset, 0)
    return placed


def gather_pieces(operand):
    if lax.axis_size("tp") != 4:
        return lax.all_gather(operand, "tp", axis=0, tiled=True)
    one = swap_tp(operand, 1)
    two = swap_tp(operand, 2)
    three = swap_tp(one, 2)
    rank = lax.axis_index("tp")
    placed = jnp.zeros((4,) + operand.shape, operand.dtype)
    for mask, part in enumerate((operand, one, two, three)):
        placed = lax.dynamic_update_slice_in_dim(placed, part[None], rank ^ mask, 0)
    return placed.reshape(-1, operand.shape[1])


def plus(mine, other):
    return mine.astype(F32) + other.astype(F32)


def hop_one(operand, other=None):
    rows = operand.shape[0] // 4
    half = rows // 2
    rank = lax.axis_index("tp")

    def part(mask, offset):
        start = (rank ^ mask) * rows + offset
        mine = lax.dynamic_slice_in_dim(operand, start, half, 0)
        if other is None:
            return mine
        return plus(mine, lax.dynamic_slice_in_dim(other, start, half, 0))

    arrived = (
        swap_tp(part(3, 0).astype(BF16), 2),
        swap_tp(part(3, half).astype(BF16), 1),
        swap_tp(part(2, 0).astype(BF16), 2),
        swap_tp(part(1, half).astype(BF16), 1),
    )
    return part, half, arrived


def hop_two(part, half, arrived):
    a3, b3, _, _ = arrived
    return (
        swap_tp(plus(part(1, 0), a3).astype(BF16), 1),
        swap_tp(plus(part(2, half), b3).astype(BF16), 2),
    )


def hop_sum(part, half, arrived, last):
    _, _, a2, b1 = arrived
    ra = plus(plus(part(0, 0), a2), last[0])
    rb = plus(plus(part(0, half), b1), last[1])
    return jnp.concatenate([ra, rb], axis=0)


def scatter_halves(operand):
    if lax.axis_size("tp") != 4:
        return lax.psum_scatter(operand, "tp", scatter_dimension=0, tiled=True).astype(F32)
    first = hop_one(operand)
    return hop_sum(*first, hop_two(*first))


def scatter_dots(operand):
    if lax.axis_size("tp") != 4:
        return lax.psum_scatter(operand, "tp", scatter_dimension=2, tiled=True)
    rank = lax.axis_index("tp")
    size = operand.shape[2] // 4
    total = lax.dynamic_slice_in_dim(operand, rank * size, size, 2)
    for mask in (1, 2, 3):
        total = total + swap_tp(
            lax.dynamic_slice_in_dim(operand, (rank ^ mask) * size, size, 2), mask
        )
    return total


def gather_small(operand):
    count = lax.axis_size("fsdp")
    nodes = count // 2
    rank = lax.axis_index("fsdp")
    node, core = rank // 2, rank % 2
    other = swap_core(operand)
    pair = jnp.where(core == 0, jnp.stack([operand, other]), jnp.stack([other, operand]))
    around = [shift_node(pair, step) for step in range(nodes - 1, 0, -1)] + [pair]
    both = jnp.concatenate(around + around, axis=0)
    placed = lax.dynamic_slice_in_dim(both, 2 * (nodes - 1 - node), count, 0)
    return placed.transpose(1, 0, 2).reshape(operand.shape[0], -1)


def reduce_small(operand):
    count = lax.axis_size("fsdp")
    nodes = count // 2
    rank = lax.axis_index("fsdp")
    node, core = rank // 2, rank % 2
    blocks = operand.reshape(operand.shape[0], nodes, 2, -1).transpose(2, 1, 0, 3)
    mine = lax.dynamic_index_in_dim(blocks, core, 0, keepdims=False)
    mine = mine + swap_core(lax.dynamic_index_in_dim(blocks, 1 - core, 0, keepdims=False))
    total = lax.dynamic_index_in_dim(mine, node, 0, keepdims=False)
    for step in range(1, nodes):
        part = lax.dynamic_index_in_dim(mine, (node + step) % nodes, 0, keepdims=False)
        total = total + shift_node(part, step)
    return sum_tp(total)


def sum_tp(operand):
    if lax.axis_size("tp") != 4:
        return lax.psum(operand, "tp")
    return (operand + swap_tp(operand, 1)) + (swap_tp(operand, 2) + swap_tp(operand, 3))


def rope_tables(positions, columns):
    halfway = columns // 2
    frequency = ROPE_BASE ** (-2.0 * jnp.arange(halfway).astype(F32) / columns)
    angles = positions.astype(F32)[:, None] * frequency[None, :]
    angles = jnp.concatenate([angles, angles], axis=-1)
    return (jnp.cos(angles)[:, None, :], jnp.sin(angles)[:, None, :])


def rotate(tensor):
    halfway = tensor.shape[-1] // 2
    return jnp.concatenate([-tensor[..., halfway:], tensor[..., :halfway]], axis=-1)


def rotate_back(tensor):
    halfway = tensor.shape[-1] // 2
    return jnp.concatenate([tensor[..., halfway:], -tensor[..., :halfway]], axis=-1)


def norm_rows(tensor):
    row_scale = lax.rsqrt(jnp.mean(tensor * tensor, axis=-1, keepdims=True) + EPSILON)
    return (tensor * row_scale, row_scale)


def norm_back(normed, row_scale, grad_normed):
    return row_scale * (
        grad_normed - normed * jnp.mean(normed * grad_normed, axis=-1, keepdims=True)
    )


def expert_kernel(extra, experts, base, *refs):
    x_ref, z_ref, gate_w, up_w, down_w = refs[:5]
    back_ref, out_ref, dots_ref, hidden_ref, gate_grad_ref, up_grad_ref, copy_ref = refs[-8:-1]
    gated_ref = refs[-1]
    count, width, size = gate_w.shape
    x = x_ref[:, :width]
    copy_ref[0] = x.T
    ends = x_ref[:, width:].astype(F32)
    lane = lax.broadcasted_iota(jnp.int32, ends.shape, 1)
    dots = jnp.zeros(ends.shape, F32)
    for e in range(count):
        columns = slice(e * size, (e + 1) * size)
        number = base[0] + e
        gate = jnp.sum(
            jnp.where((lane == number) | (lane == number + experts), ends, 0.0),
            axis=1,
            keepdims=True,
        )
        gate_pre = dot(x, gate_w[e])
        up_pre = dot(x, up_w[e])
        down_grad = z_ref[:, columns].astype(F32)
        sigmoid_gate = 1.0 / (1.0 + jnp.exp(-gate_pre))
        activated = gate_pre * sigmoid_gate
        hidden = activated * up_pre
        gated = (hidden * gate).astype(BF16)
        gated_ref[:, columns] = gated
        hidden_ref[0, columns, :] = gated.T
        dots = dots + jnp.where(
            lane == e, jnp.sum(hidden * down_grad, axis=1, keepdims=True), 0.0
        )
        hidden_grad = down_grad * gate
        gate_grad_ref[0, :, columns] = (
            hidden_grad * up_pre * sigmoid_gate * (1.0 + gate_pre * (1.0 - sigmoid_gate))
        ).astype(BF16)
        up_grad_ref[0, :, columns] = (hidden_grad * activated).astype(BF16)
    dots_ref[...] = dots
    tile = min(512, width)
    for start in range(0, width, tile):
        rows = slice(start, start + tile)
        back = jnp.zeros((x.shape[0], tile), F32)
        out = jnp.zeros((x.shape[0], tile), F32)
        for e in range(count):
            columns = slice(e * size, (e + 1) * size)
            back = back + dot_nt(gate_grad_ref[0, :, columns], gate_w[e, rows, :])
            back = back + dot_nt(up_grad_ref[0, :, columns], up_w[e, rows, :])
            out = out + dot(gated_ref[:, columns], down_w[e, :, rows])
        back_ref[:, rows] = back.astype(BF16)
        out_ref[:, rows] = out.astype(BF16)


def expert_products(base, x, z, gate_w, up_w, down_w, slots, slot, kept, experts):
    rows, wide = x.shape
    count, width, size = gate_w.shape
    extra = wide - width
    block = min(256, rows)
    hidden = count * size

    def whole(array):
        return pl.BlockSpec(
            array.shape, lambda i, base: (0, 0, 0), pipeline_mode=pl.Buffered(1)
        )

    def by_rows(columns):
        return pl.BlockSpec((block, columns), lambda i, base: (i, 0))

    def in_slot(columns):
        return pl.BlockSpec((1, block, columns), lambda i, base: (slot, i, 0))

    def turned_in_slot(columns):
        return pl.BlockSpec((1, columns, block), lambda i, base: (slot, 0, i))

    kept_shapes = [
        jax.ShapeDtypeStruct((slots, hidden, rows), BF16),
        jax.ShapeDtypeStruct((slots, rows, hidden), BF16),
        jax.ShapeDtypeStruct((slots, rows, hidden), BF16),
        jax.ShapeDtypeStruct((slots, width, rows), BF16),
    ]
    results = pl.pallas_call(
        functools.partial(expert_kernel, extra, experts),
        out_shape=[
            jax.ShapeDtypeStruct((rows, width), BF16),
            jax.ShapeDtypeStruct((rows, width), BF16),
            jax.ShapeDtypeStruct((rows, extra), F32),
        ]
        + kept_shapes,
        grid_spec=pltpu.PrefetchScalarGridSpec(
            num_scalar_prefetch=1,
            grid=(rows // block,),
            in_specs=[by_rows(wide), by_rows(hidden), whole(gate_w), whole(up_w), whole(down_w)]
            + [pl.BlockSpec(memory_space=pl.ANY)] * len(kept),
            out_specs=[by_rows(width), by_rows(width), by_rows(extra)]
            + [turned_in_slot(hidden), in_slot(hidden), in_slot(hidden), turned_in_slot(width)],
            scratch_shapes=[pltpu.VMEM((block, hidden), BF16)],
        ),
        input_output_aliases={6 + i: 3 + i for i in range(len(kept))},
        cost_estimate=pl.CostEstimate(
            flops=10 * rows * width * hidden,
            bytes_accessed=6 * width * hidden + 2 * rows * (4 * width + 4 * hidden),
            transcendentals=rows * hidden,
        ),
        compiler_params=pltpu.CompilerParams(vmem_limit_bytes=60 * 1024 * 1024),
    )(base, x, z, gate_w, up_w, down_w, *kept)
    return results[0], results[1], results[2], tuple(results[3:])


def wide_kernel(left, right, out_ref):
    count, width, size = out_ref.shape
    tile = min(512, width)
    for start in range(0, width, tile):
        rows = slice(start, start + tile)
        part = dot(left[0, rows, :], right[0])

        @pl.when(pl.program_id(0) == 0)
        def _():
            for e in range(count):
                out_ref[e, rows, :] = part[:, e * size : (e + 1) * size]

        @pl.when(pl.program_id(0) > 0)
        def _():
            for e in range(count):
                out_ref[e, rows, :] += part[:, e * size : (e + 1) * size]


def wide_products(turned, grads, count):
    slots, width, rows = turned.shape
    hidden = grads.shape[2]
    size = hidden // count
    return pl.pallas_call(
        wide_kernel,
        out_shape=jax.ShapeDtypeStruct((count, width, size), F32),
        grid=(slots,),
        in_specs=[
            pl.BlockSpec((1, width, rows), lambda k: (k, 0, 0)),
            pl.BlockSpec((1, rows, hidden), lambda k: (k, 0, 0)),
        ],
        out_specs=pl.BlockSpec((count, width, size), lambda k: (0, 0, 0)),
        cost_estimate=pl.CostEstimate(
            flops=2 * slots * rows * width * hidden,
            bytes_accessed=2 * slots * rows * (width + hidden) + 4 * width * hidden,
            transcendentals=0,
        ),
        compiler_params=pltpu.CompilerParams(vmem_limit_bytes=60 * 1024 * 1024),
    )(turned, grads)


def down_kernel(spans, has_first, left, *refs):
    out_ref = refs[-1]
    step = pl.program_id(0)
    width = out_ref.shape[1]
    tile = min(512, width)
    for index, (begin, end) in enumerate(spans):

        @pl.when((step >= begin) & (step < end))
        def _():
            for start in range(0, width, tile):
                columns = slice(start, start + tile)
                part = dot(left[0], refs[index][0, :, columns])
                if begin > 0:
                    out_ref[:, columns] += part
                elif has_first:
                    out_ref[:, columns] = refs[-2][:, columns] + part
                else:
                    out_ref[:, columns] = part


def down_products(turned, slot, arrays, first=None):
    _, hidden, rows = turned.shape
    width = arrays[0].shape[2]
    spans, count = [], 0
    for array in arrays:
        spans.append((count, count + array.shape[0]))
        count += array.shape[0]

    def member(begin, end):
        return pl.BlockSpec(
            (1, rows, width),
            lambda k: (jnp.clip(k - begin, 0, end - begin - 1), 0, 0),
            pipeline_mode=pl.Buffered(1 if end - begin == 1 else 2),
        )

    constant = pl.BlockSpec((hidden, width), lambda k: (0, 0), pipeline_mode=pl.Buffered(1))
    return pl.pallas_call(
        functools.partial(down_kernel, spans, first is not None),
        out_shape=jax.ShapeDtypeStruct((hidden, width), F32),
        grid=(count,),
        in_specs=[pl.BlockSpec((1, hidden, rows), lambda k: (slot + k, 0, 0))]
        + [member(*span) for span in spans]
        + ([constant] if first is not None else []),
        out_specs=pl.BlockSpec((hidden, width), lambda k: (0, 0)),
        cost_estimate=pl.CostEstimate(
            flops=2 * count * rows * width * hidden,
            bytes_accessed=2 * count * rows * (width + hidden) + 4 * width * hidden,
            transcendentals=0,
        ),
        compiler_params=pltpu.CompilerParams(vmem_limit_bytes=60 * 1024 * 1024),
    )(turned, *arrays, *(() if first is None else (first,)))


def swap_rows(grad):
    count = lax.axis_size("fsdp")
    core = lax.axis_index("fsdp") % 2
    blocks = grad.reshape(count // 2, 2, grad.shape[0] // count, grad.shape[1])
    return (
        lax.dynamic_index_in_dim(blocks, core, 1, keepdims=False),
        swap_core(lax.dynamic_index_in_dim(blocks, 1 - core, 1, keepdims=False)),
    )


def sum_rows(mine, arrived, *earlier):
    nodes = mine.shape[0]
    node = lax.axis_index("fsdp") // 2

    def part(step):
        place = (node + step) % nodes
        return plus(
            lax.dynamic_index_in_dim(mine, place, 0, keepdims=False),
            lax.dynamic_index_in_dim(arrived, place, 0, keepdims=False),
        )

    total, parts = part(0), []
    for step in range(1, nodes):
        parts.append(after(shift_node(part(step).astype(BF16), step), *earlier))
    for one in parts:
        total = total + one.astype(F32)
    return total


def shards(
    tokens,
    cotangent,
    routes,
    gain_attn,
    w_query,
    w_key,
    w_value,
    gain_query,
    gain_key,
    w_out,
    gain_moe,
    w_router,
    w_gate,
    w_up,
    w_down,
):
    tp_count = lax.axis_size("tp")
    tp_rank = lax.axis_index("tp")
    fsdp_count = lax.axis_size("fsdp")
    fsdp_rank = lax.axis_index("fsdp")
    nodes = fsdp_count // 2
    piece, model_width = tokens.shape
    seq_len = piece * tp_count
    local_width = w_query.shape[1]
    head_count = local_width // HEAD_DIM
    expert_count = w_router.shape[1]
    local_experts, _, hidden_slice = w_gate.shape
    hidden_all = local_experts * hidden_slice
    extra = -(-2 * expert_count // 128) * 128
    scale_factor = HEAD_DIM ** (-0.5)
    head_shape = (seq_len, head_count, HEAD_DIM)
    column_start = tp_rank * local_width

    small = gather_small(
        jnp.concatenate(
            [gain_attn[None], gain_moe[None], gain_query[None], gain_key[None], w_router.T], axis=0
        )
    )
    attn_gain, moe_gain = small[0].astype(F32), small[1].astype(F32)
    local_gains = lax.dynamic_slice_in_dim(small[2:4], column_start, local_width, 1).astype(F32)
    local_qgain, local_kgain = local_gains[0], local_gains[1]
    router_w = small[4:]
    dense_w = lax.all_gather(
        jnp.concatenate([w_query, w_key, w_value, w_out.T], axis=1), "fsdp", axis=0, tiled=True
    )
    dense_w = after(dense_w, tokens)
    qkv_w, out_w = dense_w[:, : 3 * local_width], dense_w[:, 3 * local_width :]
    down_w = w_down.reshape(hidden_all, model_width)

    residual_in = tokens.astype(F32)
    normed_one, scale_one = norm_rows(residual_in)
    first_in = (normed_one * attn_gain).astype(BF16)
    first_all = gather_halves(first_in)

    early = after(cotangent, dense_w, first_all)
    grad_own = lax.all_gather(early, "tp", axis=0, tiled=True)
    qkv_raw = dot(first_all, qkv_w)
    around = around_nodes(early, qkv_raw)
    query_raw = qkv_raw[:, :local_width]
    key_raw = qkv_raw[:, local_width : 2 * local_width]
    value_raw = qkv_raw[:, 2 * local_width :]
    squares = sum_tp(
        jnp.stack([jnp.sum(query_raw * query_raw, axis=-1), jnp.sum(key_raw * key_raw, axis=-1)])
    )
    query_scale = lax.rsqrt(squares[0] / model_width + EPSILON)[:, None]
    key_scale = lax.rsqrt(squares[1] / model_width + EPSILON)[:, None]
    positions = jnp.arange(seq_len, dtype=jnp.int32)
    cosine, sine_table = rope_tables(positions, HEAD_DIM)
    query_normed = (query_raw * query_scale * local_qgain).reshape(head_shape)
    key_normed = (key_raw * key_scale * local_kgain).reshape(head_shape)
    query_bf = (query_normed * cosine + rotate(query_normed) * sine_table).astype(BF16)
    key_bf = (key_normed * cosine + rotate(key_normed) * sine_table).astype(BF16)
    value_bf = value_raw.astype(BF16).reshape(head_shape)
    block_rows = min(512, seq_len)
    block_count = seq_len // block_rows

    def block_of(array, block_index):
        return array[block_index * block_rows : (block_index + 1) * block_rows]

    def block_scores(block_index):
        query_block = block_of(query_bf, block_index)
        scores = (
            jnp.einsum("qhd,khd->hqk", query_block, key_bf, preferred_element_type=F32)
            * scale_factor
        )
        causal = block_of(positions, block_index)[:, None] >= positions[None, :]
        return (query_block, jnp.where(causal[None], scores, -1e30), causal)

    attn_blocks, log_totals = [], []
    for block_index in range(block_count):
        query_block, scores, causal = block_scores(block_index)
        top_score = jnp.max(scores, axis=-1, keepdims=True)
        exponent = jnp.exp(scores - top_score)
        row_total = jnp.sum(exponent, axis=-1, keepdims=True)
        attn_probs = (exponent / row_total).astype(BF16)
        attn_blocks.append(
            jnp.einsum("hqk,khd->qhd", attn_probs, value_bf, preferred_element_type=F32)
        )
        log_totals.append(top_score[..., 0] + jnp.log(row_total[..., 0]))
    heads_out = jnp.concatenate(attn_blocks, axis=0).reshape(seq_len, local_width).astype(BF16)
    heads_out = after(heads_out, grad_own, *around[:1], *around[2:])
    attn_sum = scatter_halves(dot_nt(heads_out, out_w).astype(BF16))
    groups = [[0], [1, 3], [2]] if nodes == 4 else [[0]] + [list(range(1, nodes))] * (nodes > 1)
    order = [step for group in groups for step in group]

    def grad_products(own):
        other = swap_core(own)
        flat = [one.reshape(-1, model_width) for one in (own, other)]
        return (own, other) + tuple(
            dot_nt(one, down_w).astype(BF16).reshape(-1, seq_len, hidden_all) for one in flat
        )

    def grad_group(group, *earlier):
        pieces = jnp.stack([around[step - 1] for step in group])
        return grad_products(
            lax.all_gather(after(pieces, *earlier), "tp", axis=1, tiled=True)
        )

    grad_sets = [grad_products(grad_own[None])]
    if nodes > 1:
        grad_sets.append(grad_group(groups[1], attn_blocks[0]))
    hidden_res = residual_in + attn_sum
    normed_two, scale_two = norm_rows(hidden_res)
    second_in = (normed_two * moe_gain).astype(BF16)

    router_probs = jax.nn.softmax(dot_nt(second_in, router_w), axis=-1)
    own_routes = lax.dynamic_slice_in_dim(routes, tp_rank * piece, piece, 0)
    routed = jnp.any(
        own_routes[:, :, None] == jnp.arange(expert_count, dtype=jnp.int32)[None, None, :], axis=1
    ).astype(F32)
    gates = router_probs * routed
    gates_high = gates.astype(BF16)
    gates_low = (gates - gates_high.astype(F32)).astype(BF16)
    sent = jnp.concatenate(
        [
            second_in,
            gates_high,
            gates_low,
            jnp.zeros((piece, extra - 2 * expert_count), BF16),
        ],
        axis=1,
    )

    sent = after(sent, *grad_sets[0][2:])
    owns = {0: gather_halves(sent)}
    sources = around_nodes(after(sent, owns[0]))
    defer = nodes <= 4
    by_hops = tp_count == 4
    kept, gate_dots, backs, swaps, hops, lasts, returns = (), [], [], [], [], [], []
    outs, outs_back, wholes = [], [], []
    base = jnp.reshape(fsdp_rank * local_experts, (1,)).astype(jnp.int32)

    def one_sequence(place, other, rows):
        nonlocal kept
        index = next(i for i, group in enumerate(groups) if order[place] in group)
        grads = grad_sets[index][3 if other else 2][groups[index].index(order[place])]
        back, out, dots, kept = expert_products(
            base,
            rows,
            grads,
            w_gate,
            w_up,
            w_down,
            2 * nodes,
            place + (nodes if other else 0),
            kept,
            expert_count,
        )
        return back, out, dots[:, :local_experts].T

    def outputs_home(out, *earlier):
        whole = plus(out[0], swap_core(out[1])).astype(BF16)
        wholes.append(whole)
        return [
            lax.psum_scatter(after(whole, *earlier), "tp", scatter_dimension=0, tiled=True)
        ]

    for place, step in enumerate(order):
        own = owns[step]
        other = swap_core(own)
        early, late = (other, own) if 0 < place == nodes - 1 else (own, other)
        if by_hops and defer and place > 1:
            early = after(early, *lasts[place - 2], wholes[place - 2])
        if by_hops and place > 0:
            late = after(late, *hops[place - 1][2])
        if by_hops and defer and place == nodes - 1 and place > 2:
            late = after(late, returns[place - 2])
        if place == 0:
            first = one_sequence(place, False, early)
            second = one_sequence(place, True, late)
            mine, others = first, second
            for later in order[1:]:
                if later != 2:
                    owns[later] = lax.all_gather(
                        after(sources[later - 1], first[0]), "tp", axis=0, tiled=True
                    )
            if len(groups) > 2:
                grad_sets.append(grad_group(groups[2], first[0]))
            if 2 in order:
                owns[2] = lax.all_gather(
                    after(sources[1], second[0]), "tp", axis=0, tiled=True
                )
        elif place == nodes - 1:
            first = one_sequence(place, True, early)
            second = one_sequence(place, False, late)
            mine, others = second, first
        else:
            first = one_sequence(place, False, early)
            second = one_sequence(place, True, late)
            mine, others = first, second
        if place + 1 < nodes:
            owns[order[place + 1]] = after(owns[order[place + 1]], first[0])
        gate_dots.append((mine[2], others[2]))
        backs.append(mine[0])
        swaps.append(swap_core(others[0]))
        outs.append((mine[1], others[1]))
        if defer:
            out_swapped = swap_core(others[1])
            if place < nodes - 2:
                wholes.append(plus(mine[1], out_swapped).astype(BF16))
            else:
                wholes.append((mine[1], out_swapped))
        if by_hops and defer and place == nodes - 1:
            hops.append(hop_one(mine[0], swaps[-1]))
        elif by_hops:
            hops.append(hop_one(mine[0], swaps[-1]))
            lasts.append(hop_two(*hops[-1]))
            returns.append(shift_node(hop_sum(*hops[-1], lasts[-1]).astype(BF16), -step))
        else:
            back_own = plus(mine[0], swaps[-1]).astype(BF16)
            total = lax.psum_scatter(back_own, "tp", scatter_dimension=0, tiled=True)
            returns.append(shift_node(total, -step))
        if not defer:
            outs_back += [shift_node(outputs_home(outs[place])[0], -step)]
            kept = after(kept, outs_back[-1], returns[-1])
    hidden_kept, gate_kept, up_kept, rows_kept = kept

    down_w_grad = down_products(hidden_kept, 0, [one[0] for one in grad_sets])
    dots = jnp.stack([one[0] for one in gate_dots] + [one[1] for one in gate_dots], axis=1)
    dots = scatter_dots(dots)
    pins = (dots,)
    if by_hops and defer:
        part, half, arrived = hops[-1]
        arrived = tuple(after(one, down_w_grad) for one in arrived)
        last = hop_two(part, half, arrived)
        pins = arrived + (dots,)
    down_w_grad = down_products(
        after(hidden_kept, *pins), nodes, [one[1] for one in grad_sets], down_w_grad
    )
    if by_hops and defer:
        last = tuple(after(one, down_w_grad) for one in last)
        returns.append(shift_node(hop_sum(part, half, arrived, last).astype(BF16), -order[-1]))
    if defer:
        pins = last if by_hops else (returns[-1],)
        wholes = [
            plus(after(one[0], *pins), one[1]).astype(BF16)
            if isinstance(one, tuple)
            else after(one, *pins)
            for one in wholes
        ]
        pair = lax.psum_scatter(
            jnp.stack(wholes[:2]), "tp", scatter_dimension=1, tiled=True
        )
        outs_back = list(pair) + [
            lax.psum_scatter(whole, "tp", scatter_dimension=0, tiled=True)
            for whole in wholes[2:]
        ]
    back_sum = sum(one.astype(F32) for one in returns)

    def home(place, *earlier):
        if defer:
            outs_back[place] = shift_node(after(outs_back[place], *earlier), -order[place])

    node, core = fsdp_rank // 2, fsdp_rank % 2
    mine, others = dots[:, :nodes], swap_core(dots[:, nodes:])
    pair = jnp.where(core == 0, jnp.stack([mine, others]), jnp.stack([others, mine]))
    placed = jnp.stack(
        [shift_node(pair[:, :, order.index(step)], -step) for step in range(nodes)]
    )
    placed = lax.dynamic_slice_in_dim(
        jnp.concatenate([placed, placed], axis=0), nodes - node, nodes, 0
    )
    prob_grad = placed.reshape(expert_count, piece).T

    grad_out = cotangent.astype(F32)
    prob_grad = prob_grad * routed
    logit_grad = router_probs * (
        prob_grad - jnp.sum(router_probs * prob_grad, axis=-1, keepdims=True)
    )
    router_grad = lax.dot_general(
        logit_grad,
        second_in.astype(F32),
        (((0,), (0,)), ((), ())),
        precision=lax.Precision.HIGHEST,
    )
    second_grad = back_sum + jnp.dot(
        logit_grad, router_w.astype(F32), precision=lax.Precision.HIGHEST
    )
    moe_gain_grad = jnp.sum(normed_two * second_grad, axis=0)
    residual_grad = grad_out + norm_back(normed_two, scale_two, second_grad * moe_gain)

    residual_all = gather_halves(residual_grad.astype(BF16))

    gate_w_grad = wide_products(rows_kept, after(gate_kept, *returns[1:], *wholes), local_experts)
    residual_all = after(residual_all, gate_w_grad)

    out_w_swapped = swap_rows(dot_tn(residual_all, heads_out).astype(BF16))
    out_w_out = sum_rows(*out_w_swapped).T
    early_out = reduce_small(jnp.concatenate([moe_gain_grad[None], router_grad], axis=0))
    heads_grad = dot(residual_all, out_w).astype(BF16).reshape(head_shape)
    key_rot_grad = jnp.zeros(head_shape, F32)
    value_grad = jnp.zeros(head_shape, F32)
    query_blocks_grad = []
    for block_index in range(block_count):
        query_block, scores, causal = block_scores(block_index)
        log_block = log_totals[block_index]
        probs_full = jnp.where(causal[None], jnp.exp(scores - log_block[..., None]), 0.0)
        probs_bf = probs_full.astype(BF16)
        out_block = block_of(heads_grad, block_index)
        if block_index > 0:
            out_block = after(out_block, early_out, out_w_swapped[1], outs_back[0])
        value_grad = value_grad + jnp.einsum(
            "hqk,qhd->khd", probs_bf, out_block, preferred_element_type=F32
        )
        prob_block_grad = jnp.einsum(
            "qhd,khd->hqk", out_block, value_bf, preferred_element_type=F32
        )
        centre = jnp.sum(probs_full * prob_block_grad, axis=-1, keepdims=True)
        score_grad = (probs_full * (prob_block_grad - centre)).astype(BF16)
        query_blocks_grad.append(
            jnp.einsum("hqk,khd->qhd", score_grad, key_bf, preferred_element_type=F32)
            * scale_factor
        )
        key_rot_grad = (
            key_rot_grad
            + jnp.einsum("hqk,qhd->khd", score_grad, query_block, preferred_element_type=F32)
            * scale_factor
        )
    query_rot_grad = jnp.concatenate(query_blocks_grad, axis=0)
    query_norm_grad = (query_rot_grad * cosine + rotate_back(query_rot_grad * sine_table)).reshape(
        seq_len, local_width
    )
    key_norm_grad = (key_rot_grad * cosine + rotate_back(key_rot_grad * sine_table)).reshape(
        seq_len, local_width
    )
    qgain_local = jnp.sum(query_raw * query_scale * query_norm_grad, axis=0)
    kgain_local = jnp.sum(key_raw * key_scale * key_norm_grad, axis=0)
    query_inner = query_norm_grad * local_qgain
    key_inner = key_norm_grad * local_kgain
    dots = sum_tp(
        jnp.stack(
            [jnp.sum(query_raw * query_inner, axis=-1), jnp.sum(key_raw * key_inner, axis=-1)]
        )
    )
    query_raw_grad = (
        query_scale * query_inner - query_raw * query_scale**3 * dots[0][:, None] / model_width
    ).astype(BF16)
    key_raw_grad = (
        key_scale * key_inner - key_raw * key_scale**3 * dots[1][:, None] / model_width
    ).astype(BF16)
    value_raw_grad = value_grad.reshape(seq_len, local_width).astype(BF16)
    qkv_grad = jnp.concatenate([query_raw_grad, key_raw_grad, value_raw_grad], axis=1)
    qkv_grad = after(qkv_grad, out_w_out)
    first_part = dot_nt(qkv_grad, qkv_w).astype(BF16)
    first_grad = scatter_halves(first_part)
    for place in range(nodes):
        home(place, (heads_grad, heads_grad, query_blocks_grad[-1], first_grad)[min(place, 3)])
    output = (hidden_res + sum(one.astype(F32) for one in outs_back)).astype(BF16)
    qkv_w_grad = dot_tn(first_all, qkv_grad).astype(BF16)
    up_w_grad = wide_products(rows_kept, after(up_kept, first_part, qkv_w_grad), local_experts)
    down_w_grad = down_w_grad.reshape(local_experts, hidden_slice, model_width)

    attn_gain_grad = jnp.sum(normed_one * first_grad, axis=0)
    input_grad = residual_grad + norm_back(normed_one, scale_one, first_grad * attn_gain)

    qkv_out = sum_rows(*swap_rows(qkv_w_grad), up_w_grad)

    def widen(grad):
        return lax.dynamic_update_slice_in_dim(
            jnp.zeros((1, model_width), F32), grad[None], column_start, 1
        )

    late_out = reduce_small(
        jnp.concatenate(
            [attn_gain_grad[None], widen(qgain_local), widen(kgain_local)], axis=0
        )
    )
    return (
        output,
        input_grad,
        late_out[0],
        qkv_out[:, :local_width],
        qkv_out[:, local_width : 2 * local_width],
        qkv_out[:, 2 * local_width :],
        late_out[1],
        late_out[2],
        out_w_out,
        early_out[0],
        early_out[1:].T,
        gate_w_grad,
        up_w_grad,
        down_w_grad,
    )


def solution(mesh):
    placed = (
        P(("fsdp", "tp"), None),
        P(("fsdp", "tp"), None),
        P("fsdp", None),
        P("fsdp"),
        P("fsdp", "tp"),
        P("fsdp", "tp"),
        P("fsdp", "tp"),
        P("fsdp"),
        P("fsdp"),
        P("tp", "fsdp"),
        P("fsdp"),
        P("fsdp", None),
        P("fsdp", None, "tp"),
        P("fsdp", None, "tp"),
        P("fsdp", "tp", None),
    )
    return jax.shard_map(
        shards,
        mesh=mesh,
        in_specs=placed,
        out_specs=(
            P(("fsdp", "tp"), None),
            P(("fsdp", "tp"), None),
            P("fsdp"),
            P("fsdp", "tp"),
            P("fsdp", "tp"),
            P("fsdp", "tp"),
            P("fsdp"),
            P("fsdp"),
            P("tp", "fsdp"),
            P("fsdp"),
            P("fsdp", None),
            P("fsdp", None, "tp"),
            P("fsdp", None, "tp"),
            P("fsdp", "tp", None),
        ),
        check_vma=False,
    )
```
